512 devices in a mesh: prow: 16 (over z), pcol: 32 (over x, y, core).
Axes of the slice: x: 4, y: 4, z: 16, core: 2. Of those that a mesh axis runs over, the one named last changes fastest.
Arguments:
- right_sides: bfloat16 [16, 32, 3, 1, 64, 128], P('prow', 'pcol'), may hold values from -6 to 6
- lower_inverse: bfloat16 [16, 32, 3, 1, 128, 128], P('prow', 'pcol')
- upper_inverse: bfloat16 [16, 32, 3, 1, 128, 128], P('prow', 'pcol')
- lower_tiles: bfloat16 [16, 32, 2, 4, 128, 128], P('prow', 'pcol'), may hold values from -0.25 to 0.25
- lower_source: int32 [16, 32, 2, 4], P('prow', 'pcol'), may hold values from 0 to 15
- lower_target: int32 [16, 32, 2, 4], P('prow', 'pcol'), may hold values from 0 to 63, as said below
- lower_rows: int32 [16, 32, 2, 4, 128], P('prow', 'pcol'), may hold values from 0 to 128, as said below
- lower_count: int32 [16, 32, 2], P('prow', 'pcol'), may hold values from 3 to 4, as said below
- upper_tiles: bfloat16 [16, 32, 2, 4, 128, 128], P('prow', 'pcol'), may hold values from -0.25 to 0.25
- upper_source: int32 [16, 32, 2, 4], P('prow', 'pcol'), may hold values from 0 to 15
- upper_target: int32 [16, 32, 2, 4], P('prow', 'pcol'), may hold values from 0 to 63, as said below
- upper_rows: int32 [16, 32, 2, 4, 128], P('prow', 'pcol'), may hold values from 0 to 128, as said below
- upper_count: int32 [16, 32, 2], P('prow', 'pcol'), may hold values from 3 to 4, as said below
Outputs:
- solution: bfloat16 [16, 32, 3, 1, 64, 128], P('prow', 'pcol')
The draws below stay inside these ranges and needn't reach their ends.
Inputs may be any that keep to these rules, and one draw needn't show every extreme that they name: `lower_target`: in group g the value is t * 32 + i with level t < 2-g (an ancestor level). `upper_target`: in group g the value is (t - 1) * 32 + i with level t > g (a descendant level). `lower_rows`: within one block the entries below 128 are distinct; 128 marks an unused row, and every block has one or more. `upper_rows`: within one block the entries below 128 are distinct; 128 marks an unused row, and every block has one or more. `lower_count`: slots 0 to count - 1 of a group are live. `upper_count`: slots 0 to count - 1 of a group are live.
All inputs are finite; a program needn't handle non-finite values.
Results may differ from the reference program's by a relative error of at most 0.019.
Values may be sent and summed in bfloat16 or wider, within the bound.
No kernel may reach another device: no remote copies, remote signals or barrier semaphores. Data moves between devices by JAX's collectives and lax.ppermute only.
A program may use at most 64 MiB of HBM per device.

```python
import math
import jax
import jax.numpy as jnp
from jax import lax

SN = 128
NRHS = 64
LEVELS = 3
SUP_DEV = 1
BLK = 4
ROW_GROUP = 32
COL_GROUP = 16
N_PROW = 16
N_PCOL = 32


def triangle_factor(key, direction):
    layout = (N_PROW, N_PCOL, LEVELS, SUP_DEV, SN, SN)
    scales = jax.random.uniform(key, layout[:-1], jnp.float32, 0.8, 1.25)
    offdiag = jax.random.normal(jax.random.fold_in(key, 1), layout, jnp.float32) * (0.7 / math.sqrt(SN))
    positions = jnp.arange(SN)
    beyond = (positions[None, :] - positions[:, None]) * direction > 0
    identity = (positions[None, :] == positions[:, None]).astype(jnp.float32)
    return jnp.where(beyond, offdiag, 0.0) + identity * scales[..., None]


def tile_rows(key):
    layout = (N_PROW, N_PCOL, LEVELS - 1, BLK)
    scores = jax.random.randint(key, layout + (SN,), 0, 65536) * SN + jnp.arange(SN, dtype=jnp.int32)
    ordering = jnp.argsort(scores, axis=-1).astype(jnp.int32)
    unused_from = jax.random.randint(jax.random.fold_in(key, 5), layout + (1,), SN // 4, SN)
    return jnp.where(jnp.arange(SN, dtype=jnp.int32) < unused_from, ordering, SN).astype(jnp.int32)


def tile_targets(key, first_level):
    layout = (N_PROW, N_PCOL, LEVELS - 1, BLK)
    spans = LEVELS - 1 - jnp.arange(LEVELS - 1, dtype=jnp.int32)
    randoms = jax.random.randint(key, layout, 0, 1 << 20)
    offsets = randoms % spans[None, None, :, None]
    slots_drawn = jax.random.randint(jax.random.fold_in(key, 7), layout, 0, ROW_GROUP)
    encoded = (first_level[None, None, :, None] + offsets) * ROW_GROUP + slots_drawn
    encoded = encoded.at[0, 0, 0, 0].set((LEVELS - 1) * ROW_GROUP - 1)
    encoded = encoded.at[0, 0, 0, 1].set(0)
    return encoded.astype(jnp.int32)


def live_counts(key):
    layout = (N_PROW, N_PCOL, LEVELS - 1)
    loaded = jax.random.randint(key, layout, 0, 8) == 0
    lighter = jax.random.randint(jax.random.fold_in(key, 1), layout, BLK * 3 // 4, BLK + 1)
    counted = jnp.where(loaded, BLK, lighter)
    counted = counted.at[0, 0, 0].set(BLK)
    counted = counted.at[0, 0, 1].set(BLK * 3 // 4)
    return counted.astype(jnp.int32)


def draw_lower_inverse(key, part):
    key = jax.random.fold_in(key, 3)
    return triangle_factor(key, 1).astype(jnp.bfloat16)


def draw_upper_inverse(key, part):
    key = jax.random.fold_in(key, 4)
    return triangle_factor(key, -1).astype(jnp.bfloat16)


def draw_lower_target(key, part):
    key = jax.random.fold_in(key, 11)
    return tile_targets(key, jnp.zeros((LEVELS - 1,), jnp.int32))


def draw_upper_target(key, part):
    key = jax.random.fold_in(key, 12)
    return tile_targets(key, jnp.arange(LEVELS - 1, dtype=jnp.int32))


def draw_lower_rows(key, part):
    key = jax.random.fold_in(key, 21)
    return tile_rows(key)


def draw_upper_rows(key, part):
    key = jax.random.fold_in(key, 22)
    return tile_rows(key)


def draw_lower_count(key, part):
    key = jax.random.fold_in(key, 31)
    return live_counts(key)


def draw_upper_count(key, part):
    key = jax.random.fold_in(key, 32)
    return live_counts(key)


def plant(result, rng, smallest, top_value):
    index_at = [jax.random.randint(jax.random.fold_in(rng, axis), (), 0, length) for axis, length in enumerate(result.shape)]
    widest = result.shape.index(max(result.shape))
    next_to = index_at[:widest] + [(index_at[widest] + 1) % result.shape[widest]] + index_at[widest + 1:]
    return result.at[tuple(index_at)].set(smallest).at[tuple(next_to)].set(top_value)


def shard_levels(stream_key, shape, split, smallest, high):
    def one(axis_at, blocks):
        steps = jax.random.uniform(jax.random.fold_in(jax.random.fold_in(stream_key, 6), axis_at), (blocks,), jnp.float32, smallest / len(split), high / len(split))
        return jnp.repeat(jnp.exp(steps), shape[axis_at] // blocks).reshape((-1,) + (1,) * (len(shape) - axis_at - 1))

    factor_of = one(*split[0])
    for cut in split[1:]:
        factor_of = factor_of * one(*cut)
    return factor_of


def centred(stream_key, shape, width, most, cuts=(), held_as=jnp.bfloat16):
    gain = shard_levels(stream_key, shape, cuts, -0.22, 0.18) if cuts else 1.0
    array = jax.random.normal(stream_key, shape, jnp.float32) * width * gain
    return jnp.minimum(jnp.maximum(array, -most), most).astype(held_as)


def setup_inputs(seed: int = 0) -> dict:
    key_of = jax.random.split(jax.random.key(seed), 14)
    right_sides = centred(key_of[0], (N_PROW, N_PCOL, LEVELS, SUP_DEV, NRHS, SN), 1.0, 6.0, ((0, 16), (1, 32)))
    lower_inverse = draw_lower_inverse(jax.random.fold_in(key_of[13], 71), 0)
    upper_inverse = draw_upper_inverse(jax.random.fold_in(key_of[13], 71), 0)
    lower_tiles = centred(key_of[3], (N_PROW, N_PCOL, LEVELS - 1, BLK, SN, SN), (4 * SN) ** -0.5, 0.25, ((0, 16), (1, 32)))
    lower_source = plant(jax.random.randint(key_of[4], (N_PROW, N_PCOL, LEVELS - 1, BLK), 0, COL_GROUP), jax.random.fold_in(key_of[4], 1), 0, COL_GROUP - 1).astype(jnp.int32)
    lower_target = draw_lower_target(jax.random.fold_in(key_of[13], 71), 0)
    lower_rows = draw_lower_rows(jax.random.fold_in(key_of[13], 71), 0)
    lower_count = draw_lower_count(jax.random.fold_in(key_of[13], 71), 0)
    upper_tiles = centred(key_of[8], (N_PROW, N_PCOL, LEVELS - 1, BLK, SN, SN), (4 * SN) ** -0.5, 0.25, ((0, 16), (1, 32)))
    upper_source = plant(jax.random.randint(key_of[9], (N_PROW, N_PCOL, LEVELS - 1, BLK), 0, COL_GROUP), jax.random.fold_in(key_of[9], 1), 0, COL_GROUP - 1).astype(jnp.int32)
    upper_target = draw_upper_target(jax.random.fold_in(key_of[13], 71), 0)
    upper_rows = draw_upper_rows(jax.random.fold_in(key_of[13], 71), 0)
    upper_count = draw_upper_count(jax.random.fold_in(key_of[13], 71), 0)
    return dict(right_sides=right_sides, lower_inverse=lower_inverse, upper_inverse=upper_inverse, lower_tiles=lower_tiles, lower_source=lower_source, lower_target=lower_target, lower_rows=lower_rows, lower_count=lower_count, upper_tiles=upper_tiles, upper_source=upper_source, upper_target=upper_target, upper_rows=upper_rows, upper_count=upper_count)


def apply_inverse(operand, inverse):
    product = jnp.einsum("pqkns,pqkst->pqknt", operand, inverse.astype(jnp.float32), precision=lax.Precision.HIGHEST)
    return product.astype(jnp.bfloat16)


def column_tiles(solved, sources):
    grid_rows, grid_cols, per_device, side_extent, node_extent = solved.shape
    stacked = jnp.transpose(solved, (1, 0, 2, 3, 4)).reshape((grid_cols, grid_rows * per_device, side_extent, node_extent))
    columns = jnp.arange(grid_cols, dtype=jnp.int32)[None, :, None]
    return stacked[columns, sources]


def place_columns(products, row_index):
    number, extent = row_index.shape
    positions = jnp.broadcast_to(jnp.arange(extent, dtype=jnp.int32), (number, extent))
    lookup = jnp.full((number, extent + 1), extent, jnp.int32)
    lookup = lookup.at[jnp.arange(number, dtype=jnp.int32)[:, None], row_index].set(positions)[:, :extent]
    padded = jnp.pad(products, ((0, 0), (0, 0), (0, 1)))
    return jnp.take_along_axis(padded, jnp.broadcast_to(lookup[:, None, :], products.shape), axis=2)


def pick_columns(tiles, row_index):
    padded = jnp.pad(tiles, ((0, 0), (0, 0), (0, 1)))
    return jnp.take_along_axis(padded, jnp.broadcast_to(row_index[:, None, :], tiles.shape), axis=2)


def reference(right_sides, lower_inverse, upper_inverse, lower_tiles, lower_source, lower_target, lower_rows, lower_count, upper_tiles, upper_source, upper_target, upper_rows, upper_count):
    grid_rows, grid_cols, level_count, per_device, side_extent, node_extent = right_sides.shape
    row_group = per_device * grid_cols
    devices_all = grid_rows * grid_cols
    blocks = lower_tiles.shape[3]
    buffer_rows = (level_count - 1) * row_group

    def segment_rows(products, target):
        return jax.ops.segment_sum(products, target, num_segments=buffer_rows)

    def accumulate(pending, products, target, live_count):
        active = (jnp.arange(blocks, dtype=jnp.int32)[None, None, :] < live_count[:, :, None]).astype(jnp.float32)
        weighted = products * active[:, :, :, None, None]
        flat_terms = weighted.reshape((devices_all, blocks, side_extent, node_extent))
        flat_target = target.reshape((devices_all, blocks))
        summed = jax.vmap(segment_rows)(flat_terms, flat_target)
        return pending + summed.reshape((grid_rows, grid_cols, buffer_rows, side_extent, node_extent))

    def row_total(pending, height):
        piece = pending[:, :, height * row_group:(height + 1) * row_group]
        rounded = lax.optimization_barrier(piece.astype(jnp.bfloat16))
        total = jnp.sum(rounded.astype(jnp.float32), axis=1)
        return total.reshape((grid_rows, grid_cols, per_device, side_extent, node_extent))

    flat_shape = (devices_all * blocks, side_extent, node_extent)
    pending = jnp.zeros((grid_rows, grid_cols, buffer_rows, side_extent, node_extent), jnp.float32)
    forward = [None] * level_count
    for height in range(level_count - 1, -1, -1):
        operand = right_sides[:, :, height].astype(jnp.float32)
        if height < level_count - 1:
            operand = operand - row_total(pending, height)
        forward[height] = apply_inverse(operand, lower_inverse[:, :, height])
        if height > 0:
            source_group = level_count - 1 - height
            picked = column_tiles(forward[height], lower_source[:, :, source_group])
            products = jnp.einsum("pqbns,pqbst->pqbnt", picked.astype(jnp.float32), lower_tiles[:, :, source_group].astype(jnp.float32))
            moved = place_columns(products.reshape(flat_shape), lower_rows[:, :, source_group].reshape((devices_all * blocks, node_extent)))
            pending = accumulate(pending, moved.reshape(products.shape), lower_target[:, :, source_group], lower_count[:, :, source_group])

    pending = jnp.zeros((grid_rows, grid_cols, buffer_rows, side_extent, node_extent), jnp.float32)
    solution = [None] * level_count
    for height in range(level_count):
        operand = forward[height].astype(jnp.float32)
        if height > 0:
            operand = operand - row_total(pending, height - 1)
        solution[height] = apply_inverse(operand, upper_inverse[:, :, height])
        if height < level_count - 1:
            picked = column_tiles(solution[height], upper_source[:, :, height])
            chosen = pick_columns(picked.reshape(flat_shape), upper_rows[:, :, height].reshape((devices_all * blocks, node_extent)))
            chosen = chosen.reshape(picked.shape)
            products = jnp.einsum("pqbns,pqbst->pqbnt", chosen.astype(jnp.float32), upper_tiles[:, :, height].astype(jnp.float32))
            pending = accumulate(pending, products, upper_target[:, :, height], upper_count[:, :, height])
    return jnp.stack(solution, axis=2)
```

```python
import jax
import jax.numpy as jnp
from jax import lax
from jax.sharding import PartitionSpec as P


def apply_inverse(operand, inverse):
    product = jnp.einsum(
        "kns,kst->knt", operand, inverse.astype(jnp.float32), precision=lax.Precision.HIGHEST
    )
    return product.astype(jnp.bfloat16)


def select_tiles(column, source):
    selector = (source[:, None] == jnp.arange(column.shape[0], dtype=jnp.int32)[None, :]).astype(
        jnp.bfloat16
    )
    picked = jnp.einsum("bj,jns->bns", selector, column, preferred_element_type=jnp.float32)
    return picked.astype(jnp.bfloat16)


def row_table(row_index, dtype):
    extent = row_index.shape[1]
    return (row_index[:, :, None] == jnp.arange(extent, dtype=jnp.int32)[None, None, :]).astype(
        dtype
    )


def place_columns(products, row_index):
    table = row_table(row_index, jnp.float32)
    return jnp.einsum("bnp,bpq->bnq", products, table, precision=lax.Precision.HIGHEST)


def pick_columns(tiles, row_index):
    table = row_table(row_index, jnp.bfloat16)
    chosen = jnp.einsum("bnq,bpq->bnp", tiles, table, preferred_element_type=jnp.float32)
    return chosen.astype(jnp.bfloat16)


def accumulate(pending, products, target, live_count):
    blocks = products.shape[0]
    active = (jnp.arange(blocks, dtype=jnp.int32) < live_count).astype(jnp.float32)
    owners = (jnp.arange(pending.shape[0], dtype=jnp.int32)[:, None] == target[None, :]).astype(
        jnp.float32
    )
    owners = owners * active[None, :]
    return pending + jnp.einsum("tb,bnq->tnq", owners, products, precision=lax.Precision.HIGHEST)


def lower_total(partial_value):
    pieces = lax.all_to_all(partial_value.astype(jnp.bfloat16), "pcol", 0, 0, tiled=True)
    return jnp.sum(pieces.astype(jnp.float32), axis=0, keepdims=True)


def upper_total(partial_value):
    pieces = lax.all_to_all(partial_value.astype(jnp.bfloat16), "pcol", 0, 0, tiled=True)
    return jnp.sum(pieces.astype(jnp.float32), axis=0, keepdims=True)


def gather_column(tile):
    copies = jnp.broadcast_to(tile, (lax.axis_size("prow"),) + tile.shape[1:])
    return lax.all_to_all(copies, "prow", 0, 0, tiled=True)


def sweep(right_sides, factors):
    (
        lower_inverse,
        upper_inverse,
        lower_tiles,
        lower_source,
        lower_target,
        lower_rows,
        lower_count,
        upper_tiles,
        upper_source,
        upper_target,
        upper_rows,
        upper_count,
    ) = factors
    level_count, per_device, side_extent, node_extent = right_sides.shape
    row_group = per_device * lax.axis_size("pcol")
    buffer_rows = (level_count - 1) * row_group
    pending = jnp.zeros((buffer_rows, side_extent, node_extent), jnp.float32)
    forward = [None] * level_count
    for height in range(level_count - 1, -1, -1):
        operand = right_sides[height].astype(jnp.float32)
        if height < level_count - 1:
            operand = operand - lower_total(pending[height * row_group : (height + 1) * row_group])
        forward[height] = apply_inverse(operand, lower_inverse[height])
        if height > 0:
            source_group = level_count - 1 - height
            column = gather_column(forward[height])
            picked = select_tiles(column, lower_source[source_group])
            products = jnp.einsum(
                "bns,bst->bnt",
                picked,
                lower_tiles[source_group],
                preferred_element_type=jnp.float32,
            )
            moved = place_columns(products, lower_rows[source_group])
            pending = accumulate(
                pending, moved, lower_target[source_group], lower_count[source_group]
            )
    pending = jnp.zeros((buffer_rows, side_extent, node_extent), jnp.float32)
    solution = [None] * level_count
    for height in range(level_count):
        operand = forward[height].astype(jnp.float32)
        if height > 0:
            operand = operand - upper_total(pending[(height - 1) * row_group : height * row_group])
        solution[height] = apply_inverse(operand, upper_inverse[height])
        if height < level_count - 1:
            column = gather_column(solution[height])
            picked = select_tiles(column, upper_source[height])
            chosen = pick_columns(picked, upper_rows[height])
            products = jnp.einsum(
                "bns,bst->bnt", chosen, upper_tiles[height], preferred_element_type=jnp.float32
            )
            pending = accumulate(pending, products, upper_target[height], upper_count[height])
    return jnp.stack(solution, axis=0)


def body(
    right_sides,
    lower_inverse,
    upper_inverse,
    lower_tiles,
    lower_source,
    lower_target,
    lower_rows,
    lower_count,
    upper_tiles,
    upper_source,
    upper_target,
    upper_rows,
    upper_count,
):
    factors = tuple(
        (
            array[0, 0]
            for array in (
                lower_inverse,
                upper_inverse,
                lower_tiles,
                lower_source,
                lower_target,
                lower_rows,
                lower_count,
                upper_tiles,
                upper_source,
                upper_target,
                upper_rows,
                upper_count,
            )
        )
    )
    sides_local = right_sides[0, 0]
    solution = sweep(sides_local, factors)
    return solution[None, None]


def solution(mesh):
    placed = (
        P("prow", "pcol", None, None, None, None),
        P("prow", "pcol", None, None, None, None),
        P("prow", "pcol", None, None, None, None),
        P("prow", "pcol", None, None, None, None),
        P("prow", "pcol", None, None),
        P("prow", "pcol", None, None),
        P("prow", "pcol", None, None, None),
        P("prow", "pcol", None),
        P("prow", "pcol", None, None, None, None),
        P("prow", "pcol", None, None),
        P("prow", "pcol", None, None),
        P("prow", "pcol", None, None, None),
        P("prow", "pcol", None),
    )
    return jax.shard_map(
        body,
        mesh=mesh,
        in_specs=placed,
        out_specs=P("prow", "pcol", None, None, None, None),
        check_vma=False,
    )
```

```python
import jax
import jax.numpy as jnp
from jax import lax
from jax.sharding import Mesh
from jax.sharding import PartitionSpec as P

BF16 = jnp.bfloat16
F32 = jnp.float32
GROUP = ("zl", "core")
SPLIT = 4


def exact_product(operand, inverse):
    return jnp.einsum("qns,qst->qnt", operand, inverse, preferred_element_type=F32).astype(BF16)


def full_product(operand, inverse):
    return jnp.einsum(
        "qns,qst->qnt", operand, inverse.astype(F32), precision=lax.Precision.HIGHEST
    ).astype(BF16)


def moved_columns(tiles, rows):
    extent = tiles.shape[-1]
    table = (rows[..., :, None] == jnp.arange(extent, dtype=rows.dtype)).astype(BF16)
    return jnp.einsum("...sp,...pq->...sq", tiles, table, preferred_element_type=F32).astype(BF16)


def moved_rows(tiles, rows):
    extent = tiles.shape[-1]
    table = (rows[..., None, :] == jnp.arange(extent, dtype=rows.dtype)[:, None]).astype(BF16)
    return jnp.einsum("...qp,...pt->...qt", table, tiles, preferred_element_type=F32).astype(BF16)


def index_rows(source, target, live, extent):
    row = jnp.concatenate([source, target, live[None]]).astype(BF16)
    return jnp.pad(row, (0, extent - row.shape[0]))[None]


def read_index(rows, blocks):
    values = rows.astype(F32).astype(jnp.int32)
    source, target = values[:, :blocks], values[:, blocks : 2 * blocks]
    live = values[:, 2 * blocks : 2 * blocks + 1]
    active = jnp.arange(blocks, dtype=jnp.int32)[None, :] < live
    return source, jnp.where(active, target, -1)


def block_terms(column, tiles, source):
    members = jnp.arange(column.shape[0], dtype=jnp.int32)
    chosen = source[..., None] == members
    picked = jnp.zeros(source.shape + column.shape[2:], BF16)
    for j in range(column.shape[0]):
        here = chosen[..., j][..., None, None]
        picked = jnp.where(here, column[j][None, :, None], picked)
    return jnp.einsum("zcbns,zcbst->zcbnt", picked, tiles, preferred_element_type=F32)


def spread(term_groups, base, row_group):
    total = None
    slots = base + jnp.arange(row_group, dtype=jnp.int32)
    for terms, target in term_groups:
        for core in range(terms.shape[1]):
            for b in range(terms.shape[2]):
                mask = slots[:, None] == target[:, core, b][None, :]
                add = jnp.where(mask[..., None, None], terms[:, core, b][None], 0.0)
                total = add if total is None else total + add
    return total.astype(BF16)


def row_sum(partial):
    targets, pair, rows, extent = partial.shape
    cores = lax.axis_size("core")
    places = targets // cores
    chunks = partial.reshape(places, cores, pair, rows, extent)
    got = lax.all_to_all(chunks, ("x", "y"), 0, 0, tiled=True)
    total = jnp.sum(got.astype(F32), axis=0)
    return jnp.swapaxes(total, 0, 1).reshape(pair * cores, rows, extent)


def gather_column(tiles):
    copies = jnp.broadcast_to(tiles, (lax.axis_size("zh"),) + tiles.shape)
    got = lax.all_to_all(copies, "zh", 0, 0, tiled=True)
    return got.reshape((-1, lax.axis_size("core")) + tiles.shape[1:])


def body(
    right_sides,
    lower_inverse,
    upper_inverse,
    lower_tiles,
    lower_source,
    lower_target,
    lower_rows,
    lower_count,
    upper_tiles,
    upper_source,
    upper_target,
    upper_rows,
    upper_count,
):
    sides = right_sides[0, 0, :, 0]
    low_inv, up_inv = lower_inverse[0, 0, :, 0], upper_inverse[0, 0, :, 0]
    low_tiles, up_tiles = lower_tiles[0, 0], upper_tiles[0, 0]
    low_rows, up_rows = lower_rows[0, 0], upper_rows[0, 0]
    low_source, low_target, low_count = lower_source[0, 0], lower_target[0, 0], lower_count[0, 0]
    up_source, up_target, up_count = upper_source[0, 0], upper_target[0, 0], upper_count[0, 0]
    side_extent, extent = sides.shape[1:]
    blocks = low_tiles.shape[1]
    pair, cores = lax.axis_size("zl"), lax.axis_size("core")
    high = lax.axis_size("zh")
    row_group = lax.axis_size("x") * lax.axis_size("y") * cores
    rows = side_extent // SPLIT
    me = lax.axis_index("zl") * cores + lax.axis_index("core")

    late = jnp.concatenate(
        [
            low_tiles[1].reshape(-1, extent),
            up_tiles.reshape(-1, extent),
            low_inv[0],
            up_inv[0],
            up_inv[1],
            sides[0],
            low_rows[1].astype(BF16),
            up_rows.reshape(-1, extent).astype(BF16),
            index_rows(low_source[1], low_target[1], low_count[1], extent),
            index_rows(up_source[0], up_target[0], up_count[0], extent),
            index_rows(up_source[1], up_target[1], up_count[1], extent),
            jnp.zeros((1, extent), BF16),
        ],
        axis=0,
    )
    late = lax.all_gather(late, GROUP, axis=0)

    def late_tiles(at, number):
        piece = late[:, at : at + number * extent]
        return piece.reshape(pair, cores, number, extent, extent)

    forward_2 = jnp.dot(sides[2], low_inv[2], preferred_element_type=F32).astype(BF16)
    slices = forward_2.reshape(1, SPLIT, rows, extent)
    copies = jnp.broadcast_to(slices, (high,) + slices.shape[1:]).reshape(-1, rows, extent)
    column = lax.all_to_all(copies, ("zh", "zl", "core"), 0, 0, tiled=True)
    column = column.reshape(-1, cores, rows, extent)

    early = jnp.concatenate(
        [
            moved_columns(low_tiles[0], low_rows[0]).reshape(-1, extent),
            low_inv[1],
            sides[1],
            index_rows(low_source[0], low_target[0], low_count[0], extent),
            jnp.zeros((15, extent), BF16),
        ],
        axis=0,
    )
    early = lax.all_gather(early, GROUP, axis=0)
    at = blocks * extent
    tiles_l0 = early[:, :at].reshape(pair, cores, blocks, extent, extent)
    inv_l1 = early[:, at : at + extent]
    sides_1 = early[:, at + extent : at + extent + side_extent]
    index_l0 = early[:, at + extent + side_extent]

    at = blocks * extent
    raw_l1, raw_u0, raw_u1 = (late_tiles(g * at, blocks) for g in range(3))
    at = 3 * at
    inv_l0, inv_u0, inv_u1 = (late[:, at + i * extent : at + (i + 1) * extent] for i in range(3))
    at = at + 3 * extent
    sides_0 = late[:, at : at + side_extent]
    at = at + side_extent
    table = late[:, at : at + 3 * blocks].reshape(pair, cores, 3, blocks, extent)
    at = at + 3 * blocks
    index_l1, index_u0, index_u1 = (late[:, at + i] for i in range(3))
    table = table.astype(F32).astype(jnp.int32)
    tiles_l1 = moved_columns(raw_l1, table[:, :, 0])
    tiles_u0 = moved_rows(raw_u0, table[:, :, 1])
    tiles_u1 = moved_rows(raw_u1, table[:, :, 2])

    def indices(packed):
        source, target = read_index(packed, blocks)
        return source.reshape(pair, cores, blocks), target.reshape(pair, cores, blocks)

    def own_rows(tile):
        return lax.dynamic_slice_in_dim(tile, me * rows, rows, axis=1).astype(F32)

    source_l0, target_l0 = indices(index_l0)
    terms_l0 = block_terms(column, tiles_l0, source_l0)
    lower_sum = row_sum(spread([(terms_l0, target_l0)], row_group, row_group))
    forward_1 = full_product(own_rows(sides_1) - lower_sum, inv_l1)
    column = gather_column(forward_1)
    source_l1, target_l1 = indices(index_l1)
    terms_l1 = block_terms(column, tiles_l1, source_l1)
    lower_sum = row_sum(spread([(terms_l0, target_l0), (terms_l1, target_l1)], 0, row_group))
    forward_0 = full_product(own_rows(sides_0) - lower_sum, inv_l0)

    solution_0 = exact_product(forward_0, inv_u0)
    column = gather_column(solution_0)
    source_u0, target_u0 = indices(index_u0)
    terms_u0 = block_terms(column, tiles_u0, source_u0)
    upper_sum = row_sum(spread([(terms_u0, target_u0)], 0, row_group))
    solution_1 = full_product(forward_1.astype(F32) - upper_sum, inv_u1)
    column = gather_column(solution_1)

    done = lax.all_gather(jnp.stack([solution_0, solution_1], axis=1), GROUP, axis=0)
    done = lax.dynamic_index_in_dim(done, me, axis=1, keepdims=False)
    done = jnp.swapaxes(done, 0, 1).reshape(2, side_extent, extent)

    source_u1, target_u1 = indices(index_u1)
    terms_u1 = block_terms(column, tiles_u1, source_u1)
    partial = spread([(terms_u0, target_u0), (terms_u1, target_u1)], row_group, row_group)
    chunks = jnp.swapaxes(partial, 0, 1).reshape(-1, rows, extent)
    got = lax.all_to_all(chunks, ("zl", "x", "y", "core"), 0, 0, tiled=True)
    got = got.reshape(pair, row_group // cores, cores, rows, extent)
    upper_sum = jnp.sum(got.astype(F32), axis=1).reshape(side_extent, extent)
    operand = forward_2.astype(F32) - upper_sum
    solution_2 = full_product(operand[None], up_inv[2][None])
    return jnp.concatenate([done, solution_2], axis=0)[None, None, :, None]


def solution(mesh):
    z_extent = mesh.shape["prow"]
    grid = mesh.devices.reshape(z_extent // 2, 2, 4, 4, 2)
    split_mesh = Mesh(grid, ("zh", "zl", "x", "y", "core"))
    row, col = ("zh", "zl"), ("x", "y", "core")
    ranks = (6, 6, 6, 6, 4, 4, 5, 3, 6, 4, 4, 5, 3)
    placed = tuple(P(row, col, *([None] * (rank - 2))) for rank in ranks)
    return jax.shard_map(
        body,
        mesh=split_mesh,
        in_specs=placed,
        out_specs=P(row, col, None, None, None, None),
        check_vma=False,
    )
```

```python
import jax
import jax.numpy as jnp
from jax import lax
from jax.sharding import Mesh
from jax.sharding import PartitionSpec as P

BF16 = jnp.bfloat16
F32 = jnp.float32
GROUP = ("zl", "core")
SPLIT = 4
NOWHERE = 255


def exact_product(operand, inverse):
    return jnp.einsum("qns,qst->qnt", operand, inverse, preferred_element_type=F32).astype(BF16)


def full_product(operand, inverse):
    return jnp.einsum(
        "qns,qst->qnt", operand, inverse.astype(F32), precision=lax.Precision.HIGHEST
    ).astype(BF16)


def moved_columns(tiles, rows):
    extent = tiles.shape[-1]
    table = (rows[..., :, None] == jnp.arange(extent, dtype=rows.dtype)).astype(BF16)
    return jnp.einsum("...sp,...pq->...sq", tiles, table, preferred_element_type=F32).astype(BF16)


def moved_rows(tiles, rows):
    extent = tiles.shape[-1]
    table = (rows[..., None, :] == jnp.arange(extent, dtype=rows.dtype)[:, None]).astype(BF16)
    return jnp.einsum("...qp,...pt->...qt", table, tiles, preferred_element_type=F32).astype(BF16)


def gather_group(pieces):
    packed = jnp.concatenate(pieces, axis=0) if len(pieces) > 1 else pieces[0]
    return lax.all_gather(packed, GROUP, axis=0)


def beside(exchange, operand, pieces):
    packed = jnp.concatenate(pieces, axis=0) if len(pieces) > 1 else pieces[0]
    operand, packed = lax.optimization_barrier((operand, packed))
    gathered = lax.all_gather(packed, GROUP, axis=0)
    return lax.optimization_barrier((exchange(operand), gathered))


def index_rows(source, target, live):
    active = jnp.arange(source.shape[1], dtype=jnp.int32)[None, :] < live[:, None]
    return jnp.concatenate([source, jnp.where(active, target, NOWHERE)], axis=1)


def block_terms(column, tiles, source):
    picked = jnp.zeros(source.shape[:3] + column.shape[2:], BF16)
    for j in range(column.shape[0]):
        here = (source == j)[..., None, :]
        picked = jnp.where(here, column[j][None, :, None], picked)
    return jnp.einsum("zcbns,zcbst->zcbnt", picked, tiles, preferred_element_type=F32)


def spread(term_groups, base, row_group):
    total = None
    slots = (base + jnp.arange(row_group, dtype=jnp.int32)).astype(BF16)
    for terms, target in term_groups:
        for core in range(terms.shape[1]):
            for b in range(terms.shape[2]):
                mask = slots[:, None, None] == target[:, core, b][None]
                add = jnp.where(mask[:, :, None], terms[:, core, b][None], 0.0)
                total = add if total is None else total + add
    return total.astype(BF16)


def row_exchange(partial):
    targets, pair, rows, extent = partial.shape
    cores = lax.axis_size("core")
    chunks = partial.reshape(targets // cores, cores, pair, rows, extent)
    return lax.all_to_all(chunks, ("x", "y"), 0, 0, tiled=True)


def row_sum(got):
    total = jnp.sum(got.astype(F32), axis=0)
    return jnp.swapaxes(total, 0, 1).reshape((-1,) + total.shape[2:])


def gather_column(tiles):
    copies = jnp.broadcast_to(tiles, (lax.axis_size("zh"),) + tiles.shape)
    got = lax.all_to_all(copies, "zh", 0, 0, tiled=True)
    return got.reshape((-1, lax.axis_size("core")) + tiles.shape[1:])


def body(
    right_sides,
    lower_inverse,
    upper_inverse,
    lower_tiles,
    lower_source,
    lower_target,
    lower_rows,
    lower_count,
    upper_tiles,
    upper_source,
    upper_target,
    upper_rows,
    upper_count,
):
    sides = right_sides[0, 0, :, 0]
    low_inv, up_inv = lower_inverse[0, 0, :, 0], upper_inverse[0, 0, :, 0]
    low_tiles, up_tiles = lower_tiles[0, 0], upper_tiles[0, 0]
    low_rows, up_rows = lower_rows[0, 0], upper_rows[0, 0]
    low_source, low_target, low_count = lower_source[0, 0], lower_target[0, 0], lower_count[0, 0]
    up_source, up_target, up_count = upper_source[0, 0], upper_target[0, 0], upper_count[0, 0]
    side_extent, extent = sides.shape[1:]
    blocks = low_tiles.shape[1]
    pair, cores = lax.axis_size("zl"), lax.axis_size("core")
    high = lax.axis_size("zh")
    row_group = lax.axis_size("x") * lax.axis_size("y") * cores
    rows = side_extent // SPLIT
    me = lax.axis_index("zl") * cores + lax.axis_index("core")

    forward_2 = jnp.dot(sides[2], low_inv[2], preferred_element_type=F32).astype(BF16)
    slices = forward_2.reshape(1, SPLIT, rows, extent)
    copies = jnp.broadcast_to(slices, (high,) + slices.shape[1:]).reshape(-1, rows, extent)
    column = lax.all_to_all(copies, ("zh", "zl", "core"), 0, 0, tiled=True)
    column = column.reshape(-1, cores, rows, extent)

    tile_rows = blocks * extent

    def parts(gathered, *sizes):
        ends = [sum(sizes[: i + 1]) for i in range(len(sizes))]
        return [gathered[:, end - size : end] for end, size in zip(ends, sizes)]

    def as_tiles(piece):
        return piece.reshape(pair, cores, blocks, extent, extent)

    index = jnp.concatenate(
        [
            index_rows(low_source, low_target, low_count),
            index_rows(up_source, up_target, up_count),
        ],
        axis=0,
    ).astype(BF16)
    index = jnp.broadcast_to(index.reshape(-1, 1), (4 * 2 * blocks, extent))
    moved = moved_columns(low_tiles, low_rows).reshape(2, tile_rows, extent)
    moved_up = moved_rows(up_tiles, up_rows).reshape(2, tile_rows, extent)

    gathered = gather_group([moved[0], low_inv[1], sides[1], index])
    tiles_l0, inv_l1, sides_1, index = parts(gathered, tile_rows, extent, side_extent, 8 * blocks)
    tiles_l0 = as_tiles(tiles_l0)

    index = index.reshape(pair, cores, 4, 2, blocks, extent)
    sources, targets = (
        [index[:, :, group, kind] for group in range(4)] for kind in range(2)
    )

    def own_rows(tile):
        return lax.dynamic_slice_in_dim(tile, me * rows, rows, axis=1).astype(F32)

    terms_l0 = block_terms(column, tiles_l0, sources[0])
    partial = spread([(terms_l0, targets[0])], row_group, row_group)
    got, gathered = beside(row_exchange, partial, [moved[1], low_inv[0], up_inv[0], sides[0]])
    tiles_l1, inv_l0, inv_u0, sides_0 = parts(gathered, tile_rows, extent, extent, side_extent)
    forward_1 = full_product(own_rows(sides_1) - row_sum(got), inv_l1)
    column = gather_column(forward_1)
    terms_l1 = block_terms(column, as_tiles(tiles_l1), sources[1])
    partial = spread([(terms_l0, targets[0]), (terms_l1, targets[1])], 0, row_group)
    got, gathered = beside(row_exchange, partial, [moved_up[0], up_inv[1]])
    tiles_u0, inv_u1 = parts(gathered, tile_rows, extent)
    forward_0 = full_product(own_rows(sides_0) - row_sum(got), inv_l0)

    solution_0 = exact_product(forward_0, inv_u0)
    column = gather_column(solution_0)
    terms_u0 = block_terms(column, as_tiles(tiles_u0), sources[2])
    partial = spread([(terms_u0, targets[2])], 0, row_group)
    got, tiles_u1 = beside(row_exchange, partial, [moved_up[1]])
    solution_1 = full_product(forward_1.astype(F32) - row_sum(got), inv_u1)
    column = gather_column(solution_1)

    terms_u1 = block_terms(column, as_tiles(tiles_u1), sources[3])
    partial = spread([(terms_u0, targets[2]), (terms_u1, targets[3])], row_group, row_group)
    chunks = jnp.swapaxes(partial, 0, 1).reshape(-1, rows, extent)

    def home(operand):
        return lax.all_to_all(operand, ("zl", "x", "y", "core"), 0, 0, tiled=True)

    done = jnp.stack([solution_0, solution_1], axis=1)
    got, done = beside(home, chunks, [done])
    done = lax.dynamic_index_in_dim(done, me, axis=1, keepdims=False)
    done = jnp.swapaxes(done, 0, 1).reshape(2, side_extent, extent)
    got = got.reshape(pair, row_group // cores, cores, rows, extent)
    upper_sum = jnp.sum(got.astype(F32), axis=1).reshape(side_extent, extent)
    operand = forward_2.astype(F32) - upper_sum
    solution_2 = full_product(operand[None], up_inv[2][None])
    return jnp.concatenate([done, solution_2], axis=0)[None, None, :, None]


def solution(mesh):
    z_extent = mesh.shape["prow"]
    grid = mesh.devices.reshape(z_extent // 2, 2, 4, 4, 2)
    split_mesh = Mesh(grid, ("zh", "zl", "x", "y", "core"))
    row, col = ("zh", "zl"), ("x", "y", "core")
    ranks = (6, 6, 6, 6, 4, 4, 5, 3, 6, 4, 4, 5, 3)
    placed = tuple(P(row, col, *([None] * (rank - 2))) for rank in ranks)
    return jax.shard_map(
        body,
        mesh=split_mesh,
        in_specs=placed,
        out_specs=P(row, col, None, None, None, None),
        check_vma=False,
    )
```

```python
import functools

import jax
import jax.numpy as jnp
from jax import lax
from jax.experimental import pallas as pl
from jax.experimental.pallas import tpu as pltpu
from jax.sharding import Mesh
from jax.sharding import PartitionSpec as P

BF16 = jnp.bfloat16
F32 = jnp.float32
GROUP = ("zl", "core")
SPLIT = 4
NOWHERE = 255


def row_table(rows):
    places = lax.broadcasted_iota(jnp.int32, (rows.shape[-1],) * 2, 0)
    return [jnp.where(rows[b : b + 1] == places, 1.0, 0.0).astype(BF16) for b in range(rows.shape[0])]


def moved_columns(tile, table):
    return lax.dot_general(
        tile, table, (((1,), (1,)), ((), ())), preferred_element_type=F32
    ).astype(BF16)


def moved_rows(tile, table):
    return jnp.dot(table, tile, preferred_element_type=F32).astype(BF16)


def whole(array):
    return pl.BlockSpec(array.shape, lambda i: (0,) * array.ndim)


def one_of(array, place):
    return pl.BlockSpec((1,) + array.shape[1:], lambda i: (place,) + (0,) * (array.ndim - 1))


def scalars():
    return pl.BlockSpec(memory_space=pltpu.SMEM)


def first_kernel(
    sides_1, sides_2, inv_1, inv_2, tiles, rows, ls, lt, lc, us, ut, uc, packed, copies, forward, index
):
    solved = jnp.dot(sides_2[0], inv_2[0], preferred_element_type=F32).astype(BF16)
    forward[...] = solved
    for i in range(copies.shape[0]):
        copies[i] = solved
    blocks, extent = tiles.shape[1], tiles.shape[2]
    for b, table in enumerate(row_table(rows[0])):
        packed[b * extent : (b + 1) * extent] = moved_columns(tiles[0, b], table)
    at = blocks * extent
    packed[at : at + extent] = inv_1[0]
    at = at + extent
    packed[at : at + sides_1.shape[1]] = sides_1[0]
    at = at + sides_1.shape[1]
    for side, (source, target, count) in enumerate(((ls, lt, lc), (us, ut, uc))):
        for g in range(2):
            row = (2 * side + g) * 2 * blocks
            for b in range(blocks):
                goal = jnp.where(b < count[g], target[g, b], NOWHERE)
                index[row + b : row + b + 1] = jnp.full((1, extent), source[g, b], jnp.int32)
                index[row + blocks + b : row + blocks + b + 1] = jnp.full((1, extent), goal, jnp.int32)
    packed[at : at + index.shape[0]] = index[...].astype(F32).astype(BF16)


def later_kernel(sides_0, low_inv_0, up_inv_0, up_inv_1, low, up, low_rows, up_rows, start, packed):
    blocks, extent = low.shape[1], low.shape[2]
    for b, table in enumerate(row_table(low_rows[0])):
        packed[b * extent : (b + 1) * extent] = moved_columns(low[0, b], table)
    for g in range(2):
        for b, table in enumerate(row_table(up_rows[g])):
            at = ((1 + g) * blocks + b) * extent
            packed[at : at + extent] = moved_rows(up[g, b], table)
    at = 3 * blocks * extent
    for piece in (low_inv_0, up_inv_0, up_inv_1):
        packed[at : at + extent] = piece[0]
        at = at + extent
    packed[at : at + sides_0.shape[1]] = sides_0[0]


def swapped(value, axis):
    return lax.ppermute(value, axis, [(0, 1), (1, 0)])


def offsets():
    return [(step // 2, step % 2) for step in range(SPLIT)]


def spread_kernel(group, level, by_target, after, place, column, *refs):
    tiles, indices, refs = refs[:SPLIT], refs[SPLIT : 2 * SPLIT], refs[2 * SPLIT :]
    before = refs[0] if after else None
    partial, terms = refs[-2:]
    zl, core = place[0], place[1]
    extent = column.shape[3]
    rows, blocks = column.shape[2], tiles[0].shape[0] // extent
    goals = []
    for step, (dz, dc) in enumerate(offsets()):
        index = indices[step][...].astype(F32)
        half = lax.bitwise_xor(core, dc)
        held = [column[j, pl.ds(half, 1)][0].astype(F32) for j in range(column.shape[0])]
        first = 2 * blocks * group
        goals.append([index[first + blocks + b : first + blocks + b + 1] for b in range(blocks)])
        if after:
            first = first - 2 * blocks
            goals[-1] += [index[first + blocks + b : first + blocks + b + 1] for b in range(blocks)]
        first = 2 * blocks * group
        for b in range(blocks):
            source = index[first + b : first + b + 1]
            picked = jnp.zeros((rows, extent), F32)
            for j, tile in enumerate(held):
                picked = jnp.where(source == float(j), tile, picked)
            terms[step, b] = jnp.dot(
                picked.astype(BF16),
                tiles[step][b * extent : (b + 1) * extent],
                preferred_element_type=F32,
            )

    targets = partial.shape[1] if by_target else partial.shape[0]

    def one_target(t, carry):
        slot = (t + level * targets).astype(F32)
        for dz in range(2):
            total = jnp.zeros((rows, extent), F32)
            for dc in range(2):
                step = 2 * dz + dc
                for b in range(blocks):
                    total = total + jnp.where(goals[step][b] == slot, terms[step, b], 0.0)
                    if after:
                        hit = goals[step][blocks + b] == slot
                        total = total + jnp.where(hit, before[step, b], 0.0)
            row = lax.bitwise_xor(zl, dz)
            if by_target:
                partial[pl.ds(row, 1), pl.ds(t, 1)] = total.astype(BF16)[None, None]
            else:
                partial[pl.ds(t, 1), pl.ds(row, 1)] = total.astype(BF16)[None, None]
        return carry

    lax.fori_loop(0, targets, one_target, 0, unroll=4)


def full_product(operand, inverse):
    high = operand.astype(BF16)
    rest = operand - high.astype(F32)
    middle = rest.astype(BF16)
    low = (rest - middle.astype(F32)).astype(BF16)
    parts = jnp.concatenate([high, middle, low], axis=0)
    product = jnp.dot(parts, inverse, preferred_element_type=F32)
    rows = operand.shape[0]
    return product[:rows] + (product[rows : 2 * rows] + product[2 * rows :])


def solve_kernel(kind, place, got, *refs):
    inverses, refs = refs[:SPLIT], refs[SPLIT:]
    zl, core = place[0], place[1]
    rows = got.shape[3]
    me = 2 * zl + core
    if kind == 2:
        held, (solved, copies) = refs[0], refs[1:]
    elif kind == 1:
        sides, uppers, (solved, copies) = refs[:SPLIT], refs[SPLIT : 2 * SPLIT], refs[2 * SPLIT :]
    else:
        sides, (solved, copies) = refs[:SPLIT], refs[SPLIT:]
    for step, (dz, dc) in enumerate(offsets()):
        row, col = lax.bitwise_xor(zl, dz), lax.bitwise_xor(core, dc)
        total = jnp.zeros(got.shape[3:], F32)
        for i in range(got.shape[0]):
            total = total + got[i, pl.ds(col, 1), pl.ds(row, 1)][0, 0].astype(F32)
        if kind == 2:
            operand = held[step].astype(F32) - total
        else:
            mine = sides[step][pl.ds(pl.multiple_of(me * rows, rows), rows)]
            operand = mine.astype(F32) - total
        result = full_product(operand, inverses[step][...]).astype(BF16)
        if kind == 1:
            result = jnp.dot(result, uppers[step][...], preferred_element_type=F32).astype(BF16)
        solved[step] = result
        for i in range(copies.shape[0]):
            copies[i, pl.ds(row, 1), pl.ds(col, 1)] = result[None, None]


def last_kernel(place, got, forward, inverse, home_0, home_1, home_2, home_3, out):
    zl, core = place[0], place[1]
    rows = got.shape[3]
    me = 2 * zl + core
    for step, home in enumerate((home_0, home_1, home_2, home_3)):
        at = pl.multiple_of(lax.bitwise_xor(me, step) * rows, rows)
        for level in range(2):
            out[level, pl.ds(at, rows)] = home[level]
    for pair in range(got.shape[0]):
        for core_at in range(got.shape[2]):
            total = jnp.zeros(got.shape[3:], F32)
            for i in range(got.shape[1]):
                total = total + got[pair, i, core_at].astype(F32)
            at = (2 * pair + core_at) * rows
            operand = forward[at : at + rows].astype(F32) - total
            out[2, at : at + rows] = full_product(operand, inverse[0]).astype(BF16)


def row_exchange(partial):
    cores = lax.axis_size("core")
    chunks = partial.reshape((-1, cores) + partial.shape[1:])
    return lax.all_to_all(chunks, ("x", "y"), 0, 0, tiled=True)


def gather_column(copies):
    got = lax.all_to_all(copies, "zh", 0, 0, tiled=True)
    return got.reshape((-1,) + got.shape[2:])


def body(
    right_sides,
    lower_inverse,
    upper_inverse,
    lower_tiles,
    lower_source,
    lower_target,
    lower_rows,
    lower_count,
    upper_tiles,
    upper_source,
    upper_target,
    upper_rows,
    upper_count,
):
    sides = right_sides[0, 0, :, 0]
    low_inv, up_inv = lower_inverse[0, 0, :, 0], upper_inverse[0, 0, :, 0]
    low_tiles, up_tiles = lower_tiles[0, 0], upper_tiles[0, 0]
    low_rows, up_rows = lower_rows[0, 0], upper_rows[0, 0]
    low_source, low_target, low_count = lower_source[0, 0], lower_target[0, 0], lower_count[0, 0]
    up_source, up_target, up_count = upper_source[0, 0], upper_target[0, 0], upper_count[0, 0]
    side_extent, extent = sides.shape[1:]
    blocks = low_tiles.shape[1]
    pair, cores = lax.axis_size("zl"), lax.axis_size("core")
    high = lax.axis_size("zh")
    row_group = lax.axis_size("x") * lax.axis_size("y") * cores
    rows = side_extent // SPLIT
    tile_rows = blocks * extent

    first_sizes = [tile_rows, extent, side_extent, 8 * blocks]
    packed, copies, forward_2 = pl.pallas_call(
        first_kernel,
        grid=(1,),
        in_specs=[one_of(sides, 1), one_of(sides, 2), one_of(low_inv, 1), one_of(low_inv, 2)]
        + [one_of(low_tiles, 0), one_of(low_rows, 0)]
        + [scalars()] * 6,
        out_shape=[
            jax.ShapeDtypeStruct((sum(first_sizes), extent), BF16),
            jax.ShapeDtypeStruct((high, side_extent, extent), BF16),
            jax.ShapeDtypeStruct((side_extent, extent), BF16),
        ],
        out_specs=[
            pl.BlockSpec((sum(first_sizes), extent), lambda i: (0, 0)),
            pl.BlockSpec((high, side_extent, extent), lambda i: (0, 0, 0)),
            pl.BlockSpec((side_extent, extent), lambda i: (0, 0)),
        ],
        scratch_shapes=[pltpu.VMEM((8 * blocks, extent), jnp.int32)],
        compiler_params=pltpu.CompilerParams(vmem_limit_bytes=16 << 20),
    )(
        *(sides, sides, low_inv, low_inv, low_tiles, low_rows),
        *(low_source, low_target, low_count, up_source, up_target, up_count),
    )
    z_mate = swapped(packed, "zl")
    copies = copies.reshape(-1, rows, extent)
    column = lax.all_to_all(copies, ("zh", "zl", "core"), 0, 0, tiled=True)
    column = column.reshape(-1, cores, rows, extent)
    packed, z_mate = lax.optimization_barrier((packed, z_mate))
    first = (packed, swapped(packed, "core"), z_mate, swapped(z_mate, "core"))

    later_sizes = [tile_rows] * 3 + [extent] * 3 + [side_extent]
    start = first[3][:16]
    packed = pl.pallas_call(
        later_kernel,
        grid=(1,),
        in_specs=[one_of(sides, 0), one_of(low_inv, 0), one_of(up_inv, 0), one_of(up_inv, 1)]
        + [one_of(low_tiles, 1), whole(up_tiles), one_of(low_rows, 1), whole(up_rows), whole(start)],
        out_shape=jax.ShapeDtypeStruct((sum(later_sizes), extent), BF16),
        out_specs=pl.BlockSpec((sum(later_sizes), extent), lambda i: (0, 0)),
        compiler_params=pltpu.CompilerParams(vmem_limit_bytes=16 << 20),
    )(sides, low_inv, up_inv, up_inv, low_tiles, up_tiles, low_rows, up_rows, start)
    z_mate = swapped(packed, "zl")
    later = (packed, swapped(packed, "core"), z_mate, swapped(z_mate, "core"))

    place = jnp.stack([lax.axis_index("zl"), lax.axis_index("core")]).astype(jnp.int32)

    def rows_of(sizes, number):
        start, size = sum(sizes[:number]), sizes[number]
        return pl.BlockSpec((size, extent), lambda i: (start // size, 0))

    index_block = rows_of(first_sizes, 3)

    def edge(column, buffers, tile_block, group, level, before=None, by_target=False):
        shape = (row_group, pair) if not by_target else (pair, row_group)
        partial = jax.ShapeDtypeStruct(shape + (rows, extent), BF16)
        terms = jax.ShapeDtypeStruct((SPLIT, blocks, rows, extent), F32)
        extra = () if before is None else (before,)
        return pl.pallas_call(
            functools.partial(spread_kernel, group, level, by_target, before is not None),
            grid=(1,),
            in_specs=[scalars(), whole(column)]
            + [tile_block] * SPLIT
            + [index_block] * SPLIT
            + [whole(array) for array in extra],
            out_shape=[partial, terms],
            out_specs=[whole(partial), whole(terms)],
            compiler_params=pltpu.CompilerParams(vmem_limit_bytes=16 << 20),
        )(place, column, *buffers, *first, *extra)

    def solve(kind, got, *pieces):
        solved = jax.ShapeDtypeStruct((SPLIT, rows, extent), BF16)
        copies = jax.ShapeDtypeStruct((high, pair, cores, rows, extent), BF16)
        arrays, specs = [], []
        for buffers, block in pieces:
            arrays += buffers
            specs += [block] * len(buffers)
        return pl.pallas_call(
            functools.partial(solve_kernel, kind),
            grid=(1,),
            in_specs=[scalars(), whole(got)] + specs,
            out_shape=[solved, copies],
            out_specs=[whole(solved), whole(copies)],
            compiler_params=pltpu.CompilerParams(vmem_limit_bytes=16 << 20),
        )(place, got, *arrays)

    partial, terms = edge(column, first, rows_of(first_sizes, 0), 0, 1)
    got = row_exchange(partial)
    inverse, side = rows_of(first_sizes, 1), rows_of(first_sizes, 2)
    forward_1, copies = solve(0, got, (first, inverse), (first, side))
    column = gather_column(copies)
    partial, _ = edge(column, later, rows_of(later_sizes, 0), 1, 0, terms)
    got = row_exchange(partial)
    inverse, upper, side = (rows_of(later_sizes, i) for i in (3, 4, 6))
    solution_0, copies = solve(1, got, (later, inverse), (later, side), (later, upper))

    column = gather_column(copies)
    partial, terms = edge(column, later, rows_of(later_sizes, 1), 2, 0)
    got = row_exchange(partial)
    solution_1, copies = solve(2, got, (later, rows_of(later_sizes, 5)), ([forward_1], whole(forward_1)))
    column = gather_column(copies)

    done = jnp.stack([solution_0, solution_1], axis=1)
    home = [done[0]]
    for step in range(1, SPLIT):
        home.append(lax.ppermute(done[step], GROUP, [(i, i ^ step) for i in range(SPLIT)]))
    column, *home = lax.optimization_barrier((column, *home))
    partial, _ = edge(column, later, rows_of(later_sizes, 2), 3, 1, terms, by_target=True)
    got = lax.all_to_all(partial.reshape(-1, rows, extent), ("zl", "x", "y", "core"), 0, 0, tiled=True)
    got = got.reshape(pair, row_group // cores, cores, rows, extent)
    result = jax.ShapeDtypeStruct(sides.shape, BF16)
    result = pl.pallas_call(
        last_kernel,
        grid=(1,),
        in_specs=[scalars(), whole(got), whole(forward_2), one_of(up_inv, 2)]
        + [whole(piece) for piece in home],
        out_shape=result,
        out_specs=whole(result),
        compiler_params=pltpu.CompilerParams(vmem_limit_bytes=16 << 20),
    )(place, got, forward_2, up_inv, *home)
    return result[None, None, :, None]


def solution(mesh):
    z_extent = mesh.shape["prow"]
    grid = mesh.devices.reshape(z_extent // 2, 2, 4, 4, 2)
    split_mesh = Mesh(grid, ("zh", "zl", "x", "y", "core"))
    row, col = ("zh", "zl"), ("x", "y", "core")
    ranks = (6, 6, 6, 6, 4, 4, 5, 3, 6, 4, 4, 5, 3)
    placed = tuple(P(row, col, *([None] * (rank - 2))) for rank in ranks)
    return jax.shard_map(
        body,
        mesh=split_mesh,
        in_specs=placed,
        out_specs=P(row, col, None, None, None, None),
        check_vma=False,
    )
```

```python
import functools

import jax
import jax.numpy as jnp
from jax import lax
from jax.experimental import pallas as pl
from jax.experimental.pallas import tpu as pltpu
from jax.sharding import Mesh
from jax.sharding import PartitionSpec as P

BF16 = jnp.bfloat16
F32 = jnp.float32
GROUP = ("zl", "core")
SPLIT = 4
NOWHERE = 255


def row_table(rows):
    places = lax.broadcasted_iota(jnp.int32, (rows.shape[-1],) * 2, 0)
    return [jnp.where(rows[b : b + 1] == places, 1.0, 0.0).astype(BF16) for b in range(rows.shape[0])]


def moved_columns(tile, table):
    return lax.dot_general(
        tile, table, (((1,), (1,)), ((), ())), preferred_element_type=F32
    ).astype(BF16)


def moved_rows(tile, table):
    return jnp.dot(table, tile, preferred_element_type=F32).astype(BF16)


def whole(array):
    return pl.BlockSpec(array.shape, lambda i: (0,) * array.ndim)


def one_of(array, place):
    return pl.BlockSpec((1,) + array.shape[1:], lambda i: (place,) + (0,) * (array.ndim - 1))


def scalars():
    return pl.BlockSpec(memory_space=pltpu.SMEM)


def top_kernel(sides, inverse, copies, forward):
    solved = jnp.dot(sides[0], inverse[0], preferred_element_type=F32).astype(BF16)
    forward[...] = solved
    for i in range(copies.shape[0]):
        copies[i] = solved


def first_kernel(sides_1, inv_1, tiles, rows, ls, lt, lc, us, ut, uc, packed, index):
    blocks, extent = tiles.shape[1], tiles.shape[2]
    for b, table in enumerate(row_table(rows[0])):
        packed[b * extent : (b + 1) * extent] = moved_columns(tiles[0, b], table)
    at = blocks * extent
    packed[at : at + extent] = inv_1[0]
    at = at + extent
    packed[at : at + sides_1.shape[1]] = sides_1[0]
    at = at + sides_1.shape[1]
    for side, (source, target, count) in enumerate(((ls, lt, lc), (us, ut, uc))):
        for g in range(2):
            row = (2 * side + g) * 2 * blocks
            for b in range(blocks):
                goal = jnp.where(b < count[g], target[g, b], NOWHERE)
                index[row + b : row + b + 1] = jnp.full((1, extent), source[g, b], jnp.int32)
                index[row + blocks + b : row + blocks + b + 1] = jnp.full((1, extent), goal, jnp.int32)
    packed[at : at + index.shape[0]] = index[...].astype(F32).astype(BF16)


def later_kernel(sides_0, low_inv_0, up_inv_0, up_inv_1, low, up, low_rows, up_rows, start, packed):
    blocks, extent = low.shape[1], low.shape[2]
    for b, table in enumerate(row_table(low_rows[0])):
        packed[b * extent : (b + 1) * extent] = moved_columns(low[0, b], table)
    for g in range(2):
        for b, table in enumerate(row_table(up_rows[g])):
            at = ((1 + g) * blocks + b) * extent
            packed[at : at + extent] = moved_rows(up[g, b], table)
    at = 3 * blocks * extent
    for piece in (low_inv_0, up_inv_0, up_inv_1):
        packed[at : at + extent] = piece[0]
        at = at + extent
    packed[at : at + sides_0.shape[1]] = sides_0[0]


def swapped(value, axis):
    return lax.ppermute(value, axis, [(0, 1), (1, 0)])


def offsets():
    return [(step // 2, step % 2) for step in range(SPLIT)]


def spread_kernel(group, level, by_target, after, place, column, *refs):
    tiles, indices, refs = refs[:SPLIT], refs[SPLIT : 2 * SPLIT], refs[2 * SPLIT :]
    before = refs[0] if after else None
    partial, terms = refs[-2:]
    zl, core = place[0], place[1]
    extent = column.shape[3]
    rows, blocks = column.shape[2], tiles[0].shape[0] // extent
    goals = []
    for step, (dz, dc) in enumerate(offsets()):
        index = indices[step][...].astype(F32)
        half = lax.bitwise_xor(core, dc)
        held = [column[j, pl.ds(half, 1)][0].astype(F32) for j in range(column.shape[0])]
        first = 2 * blocks * group
        goals.append([index[first + blocks + b : first + blocks + b + 1] for b in range(blocks)])
        if after:
            first = first - 2 * blocks
            goals[-1] += [index[first + blocks + b : first + blocks + b + 1] for b in range(blocks)]
        first = 2 * blocks * group
        for b in range(blocks):
            source = index[first + b : first + b + 1]
            picked = jnp.zeros((rows, extent), F32)
            for j, tile in enumerate(held):
                picked = jnp.where(source == float(j), tile, picked)
            terms[step, b] = jnp.dot(
                picked.astype(BF16),
                tiles[step][b * extent : (b + 1) * extent],
                preferred_element_type=F32,
            )

    targets = partial.shape[1] if by_target else partial.shape[0]

    def one_target(t, carry):
        slot = (t + level * targets).astype(F32)
        for dz in range(2):
            total = jnp.zeros((rows, extent), F32)
            for dc in range(2):
                step = 2 * dz + dc
                for b in range(blocks):
                    total = total + jnp.where(goals[step][b] == slot, terms[step, b], 0.0)
                    if after:
                        hit = goals[step][blocks + b] == slot
                        total = total + jnp.where(hit, before[step, b], 0.0)
            row = lax.bitwise_xor(zl, dz)
            if by_target:
                partial[pl.ds(row, 1), pl.ds(t, 1)] = total.astype(BF16)[None, None]
            else:
                partial[pl.ds(t, 1), pl.ds(row, 1)] = total.astype(BF16)[None, None]
        return carry

    lax.fori_loop(0, targets, one_target, 0, unroll=4)


def scatter_kernel(group, level, by_target, after, place, table, column, *refs):
    tiles, before = refs[:SPLIT], refs[SPLIT] if after else None
    partial, terms, sums = (refs[-2], None, refs[-1]) if after else refs[-3:]
    zl, core = place[0], place[1]
    extent = column.shape[3]
    blocks = tiles[0].shape[0] // extent
    targets = partial.shape[1] if by_target else partial.shape[0]
    sums[...] = jnp.zeros(sums.shape, F32)

    def add(step, entry, row, term):
        goal = table[step, entry] - level * targets
        slot = jnp.where((goal >= 0) & (goal < targets), goal, targets)
        at = (pl.ds(row, 1), pl.ds(slot, 1)) if by_target else (pl.ds(slot, 1), pl.ds(row, 1))
        sums[at] = sums[at] + term[None, None]

    for step, (dz, dc) in enumerate(offsets()):
        half, row = lax.bitwise_xor(core, dc), lax.bitwise_xor(zl, dz)
        for b in range(blocks):
            source = jnp.clip(table[step, 2 * blocks * group + b], 0, column.shape[0] - 1)
            term = jnp.dot(
                column[pl.ds(source, 1), pl.ds(half, 1)][0, 0],
                tiles[step][b * extent : (b + 1) * extent],
                preferred_element_type=F32,
            )
            if not after:
                terms[step, b] = term
            add(step, 2 * blocks * group + blocks + b, row, term)
            if after:
                add(step, 2 * blocks * (group - 1) + blocks + b, row, before[step, b])
    partial[...] = (sums[:, :targets] if by_target else sums[:targets]).astype(BF16)


def full_product(operand, inverse):
    high = operand.astype(BF16)
    rest = operand - high.astype(F32)
    middle = rest.astype(BF16)
    low = (rest - middle.astype(F32)).astype(BF16)
    parts = jnp.concatenate([high, middle, low], axis=0)
    product = jnp.dot(parts, inverse, preferred_element_type=F32)
    rows = operand.shape[0]
    return product[:rows] + (product[rows : 2 * rows] + product[2 * rows :])


def solve_kernel(kind, place, got, *refs):
    inverses, refs = refs[:SPLIT], refs[SPLIT:]
    zl, core = place[0], place[1]
    rows = got.shape[3]
    me = 2 * zl + core
    if kind == 2:
        held, (solved, copies) = refs[0], refs[1:]
    elif kind == 1:
        sides, uppers, (solved, copies) = refs[:SPLIT], refs[SPLIT : 2 * SPLIT], refs[2 * SPLIT :]
    else:
        sides, (solved, copies) = refs[:SPLIT], refs[SPLIT:]
    for step, (dz, dc) in enumerate(offsets()):
        row, col = lax.bitwise_xor(zl, dz), lax.bitwise_xor(core, dc)
        total = jnp.zeros(got.shape[3:], F32)
        for i in range(got.shape[0]):
            total = total + got[i, pl.ds(col, 1), pl.ds(row, 1)][0, 0].astype(F32)
        if kind == 2:
            operand = held[step].astype(F32) - total
        else:
            mine = sides[step][pl.ds(pl.multiple_of(me * rows, rows), rows)]
            operand = mine.astype(F32) - total
        result = full_product(operand, inverses[step][...]).astype(BF16)
        if kind == 1:
            result = jnp.dot(result, uppers[step][...], preferred_element_type=F32).astype(BF16)
        solved[step] = result
        for i in range(copies.shape[0]):
            copies[i, pl.ds(row, 1), pl.ds(col, 1)] = result[None, None]


def last_kernel(place, got, forward, inverse, home_0, home_1, home_2, home_3, out):
    zl, core = place[0], place[1]
    rows = got.shape[3]
    me = 2 * zl + core
    for step, home in enumerate((home_0, home_1, home_2, home_3)):
        at = pl.multiple_of(lax.bitwise_xor(me, step) * rows, rows)
        for level in range(2):
            out[level, pl.ds(at, rows)] = home[level]
    for pair in range(got.shape[0]):
        for core_at in range(got.shape[2]):
            total = jnp.zeros(got.shape[3:], F32)
            for i in range(got.shape[1]):
                total = total + got[pair, i, core_at].astype(F32)
            at = (2 * pair + core_at) * rows
            operand = forward[at : at + rows].astype(F32) - total
            out[2, at : at + rows] = full_product(operand, inverse[0]).astype(BF16)


def row_exchange(partial):
    cores = lax.axis_size("core")
    chunks = partial.reshape((-1, cores) + partial.shape[1:])
    return lax.all_to_all(chunks, ("x", "y"), 0, 0, tiled=True)


def gather_column(copies):
    got = lax.all_to_all(copies, "zh", 0, 0, tiled=True)
    return got.reshape((-1,) + got.shape[2:])


def body(
    right_sides,
    lower_inverse,
    upper_inverse,
    lower_tiles,
    lower_source,
    lower_target,
    lower_rows,
    lower_count,
    upper_tiles,
    upper_source,
    upper_target,
    upper_rows,
    upper_count,
):
    sides = right_sides[0, 0, :, 0]
    low_inv, up_inv = lower_inverse[0, 0, :, 0], upper_inverse[0, 0, :, 0]
    low_tiles, up_tiles = lower_tiles[0, 0], upper_tiles[0, 0]
    low_rows, up_rows = lower_rows[0, 0], upper_rows[0, 0]
    low_source, low_target, low_count = lower_source[0, 0], lower_target[0, 0], lower_count[0, 0]
    up_source, up_target, up_count = upper_source[0, 0], upper_target[0, 0], upper_count[0, 0]
    side_extent, extent = sides.shape[1:]
    blocks = low_tiles.shape[1]
    pair, cores = lax.axis_size("zl"), lax.axis_size("core")
    high = lax.axis_size("zh")
    row_group = lax.axis_size("x") * lax.axis_size("y") * cores
    rows = side_extent // SPLIT
    tile_rows = blocks * extent

    first_sizes = [tile_rows, extent, side_extent, 8 * blocks]
    copies, forward_2 = pl.pallas_call(
        top_kernel,
        grid=(1,),
        in_specs=[one_of(sides, 2), one_of(low_inv, 2)],
        out_shape=[
            jax.ShapeDtypeStruct((high, side_extent, extent), BF16),
            jax.ShapeDtypeStruct((side_extent, extent), BF16),
        ],
        out_specs=[
            pl.BlockSpec((high, side_extent, extent), lambda i: (0, 0, 0)),
            pl.BlockSpec((side_extent, extent), lambda i: (0, 0)),
        ],
        compiler_params=pltpu.CompilerParams(vmem_limit_bytes=56 << 20),
    )(sides, low_inv)
    packed = pl.pallas_call(
        first_kernel,
        grid=(1,),
        in_specs=[one_of(sides, 1), one_of(low_inv, 1), one_of(low_tiles, 0), one_of(low_rows, 0)]
        + [scalars()] * 6,
        out_shape=jax.ShapeDtypeStruct((sum(first_sizes), extent), BF16),
        out_specs=pl.BlockSpec((sum(first_sizes), extent), lambda i: (0, 0)),
        scratch_shapes=[pltpu.VMEM((8 * blocks, extent), jnp.int32)],
        compiler_params=pltpu.CompilerParams(vmem_limit_bytes=16 << 20),
    )(
        *(sides, low_inv, low_tiles, low_rows),
        *(low_source, low_target, low_count, up_source, up_target, up_count),
    )
    z_mate = swapped(packed, "zl")
    copies = copies.reshape(-1, rows, extent)
    column = lax.all_to_all(copies, ("zh", "zl", "core"), 0, 0, tiled=True)
    column = column.reshape(-1, cores, rows, extent)
    first = (packed, swapped(packed, "core"), z_mate, swapped(z_mate, "core"))

    later_sizes = [tile_rows] * 3 + [extent] * 3 + [side_extent]
    start = packed[:16]
    packed = pl.pallas_call(
        later_kernel,
        grid=(1,),
        in_specs=[one_of(sides, 0), one_of(low_inv, 0), one_of(up_inv, 0), one_of(up_inv, 1)]
        + [one_of(low_tiles, 1), whole(up_tiles), one_of(low_rows, 1), whole(up_rows), whole(start)],
        out_shape=jax.ShapeDtypeStruct((sum(later_sizes), extent), BF16),
        out_specs=pl.BlockSpec((sum(later_sizes), extent), lambda i: (0, 0)),
        compiler_params=pltpu.CompilerParams(vmem_limit_bytes=16 << 20),
    )(sides, low_inv, up_inv, up_inv, low_tiles, up_tiles, low_rows, up_rows, start)
    z_mate = swapped(packed, "zl")
    later = (packed, swapped(packed, "core"), z_mate, swapped(z_mate, "core"))

    place = jnp.stack([lax.axis_index("zl"), lax.axis_index("core")]).astype(jnp.int32)

    def rows_of(sizes, number):
        start, size = sum(sizes[:number]), sizes[number]
        return pl.BlockSpec((size, extent), lambda i: (start // size, 0))

    index_block = rows_of(first_sizes, 3)

    table = jnp.stack([buffer[-8 * blocks :, 0] for buffer in first])
    table = table.astype(F32).astype(jnp.int32)

    def edge(column, buffers, tile_block, group, level, before=None, by_target=False):
        shape = (row_group, pair) if not by_target else (pair, row_group)
        partial = jax.ShapeDtypeStruct(shape + (rows, extent), BF16)
        terms = jax.ShapeDtypeStruct((SPLIT, blocks, rows, extent), F32)
        extra = () if before is None else (before,)
        extra_specs = [whole(array) for array in extra]
        if group == 0:
            kernel, scratch = spread_kernel, []
            in_specs = [scalars(), whole(column)] + [tile_block] * SPLIT + [index_block] * SPLIT
            arrays = (place, column, *buffers, *first)
        else:
            kernel = scatter_kernel
            sums = (row_group + 1, pair) if not by_target else (pair, row_group + 1)
            scratch = [pltpu.VMEM(sums + (rows, extent), F32)]
            in_specs = [scalars(), scalars(), whole(column)] + [tile_block] * SPLIT
            arrays = (place, table, column, *buffers)
        return pl.pallas_call(
            functools.partial(kernel, group, level, by_target, before is not None),
            grid=(1,),
            in_specs=in_specs + extra_specs,
            out_shape=[partial, terms] if before is None else [partial],
            out_specs=[whole(partial), whole(terms)] if before is None else [whole(partial)],
            scratch_shapes=scratch,
            compiler_params=pltpu.CompilerParams(vmem_limit_bytes=16 << 20),
        )(*arrays, *extra)

    def solve(kind, got, *pieces):
        solved = jax.ShapeDtypeStruct((SPLIT, rows, extent), BF16)
        copies = jax.ShapeDtypeStruct((high, pair, cores, rows, extent), BF16)
        arrays, specs = [], []
        for buffers, block in pieces:
            arrays += buffers
            specs += [block] * len(buffers)
        return pl.pallas_call(
            functools.partial(solve_kernel, kind),
            grid=(1,),
            in_specs=[scalars(), whole(got)] + specs,
            out_shape=[solved, copies],
            out_specs=[whole(solved), whole(copies)],
            compiler_params=pltpu.CompilerParams(vmem_limit_bytes=16 << 20),
        )(place, got, *arrays)

    partial, terms = edge(column, first, rows_of(first_sizes, 0), 0, 1)
    got = row_exchange(partial)
    inverse, side = rows_of(first_sizes, 1), rows_of(first_sizes, 2)
    forward_1, copies = solve(0, got, (first, inverse), (first, side))
    column = gather_column(copies)
    (partial,) = edge(column, later, rows_of(later_sizes, 0), 1, 0, terms)
    got = row_exchange(partial)
    inverse, upper, side = (rows_of(later_sizes, i) for i in (3, 4, 6))
    solution_0, copies = solve(1, got, (later, inverse), (later, side), (later, upper))

    column = gather_column(copies)
    partial, terms = edge(column, later, rows_of(later_sizes, 1), 2, 0)
    got = row_exchange(partial)
    solution_1, copies = solve(2, got, (later, rows_of(later_sizes, 5)), ([forward_1], whole(forward_1)))
    column = gather_column(copies)

    done = jnp.stack([solution_0, solution_1], axis=1)
    home = [done[0]]
    for step in range(1, SPLIT):
        home.append(lax.ppermute(done[step], GROUP, [(i, i ^ step) for i in range(SPLIT)]))
    column, *home = lax.optimization_barrier((column, *home))
    (partial,) = edge(column, later, rows_of(later_sizes, 2), 3, 1, terms, by_target=True)
    got = lax.all_to_all(partial.reshape(-1, rows, extent), ("zl", "x", "y", "core"), 0, 0, tiled=True)
    got = got.reshape(pair, row_group // cores, cores, rows, extent)
    result = jax.ShapeDtypeStruct(sides.shape, BF16)
    result = pl.pallas_call(
        last_kernel,
        grid=(1,),
        in_specs=[scalars(), whole(got), whole(forward_2), one_of(up_inv, 2)]
        + [whole(piece) for piece in home],
        out_shape=result,
        out_specs=whole(result),
        compiler_params=pltpu.CompilerParams(vmem_limit_bytes=16 << 20),
    )(place, got, forward_2, up_inv, *home)
    return result[None, None, :, None]


def solution(mesh):
    z_extent = mesh.shape["prow"]
    grid = mesh.devices.reshape(z_extent // 2, 2, 4, 4, 2)
    split_mesh = Mesh(grid, ("zh", "zl", "x", "y", "core"))
    row, col = ("zh", "zl"), ("x", "y", "core")
    ranks = (6, 6, 6, 6, 4, 4, 5, 3, 6, 4, 4, 5, 3)
    placed = tuple(P(row, col, *([None] * (rank - 2))) for rank in ranks)
    return jax.shard_map(
        body,
        mesh=split_mesh,
        in_specs=placed,
        out_specs=P(row, col, None, None, None, None),
        check_vma=False,
    )
```

```python
import functools

import jax
import jax.numpy as jnp
from jax import lax
from jax.experimental import pallas as pl
from jax.experimental.pallas import tpu as pltpu
from jax.sharding import Mesh
from jax.sharding import PartitionSpec as P

BF16 = jnp.bfloat16
F32 = jnp.float32
GROUP = ("zl", "core")
SPLIT = 4
NOWHERE = 255


def row_table(rows):
    places = lax.broadcasted_iota(jnp.int32, (rows.shape[-1],) * 2, 0)
    return [jnp.where(rows[b : b + 1] == places, 1.0, 0.0).astype(BF16) for b in range(rows.shape[0])]


def moved_columns(tile, table):
    return lax.dot_general(
        tile, table, (((1,), (1,)), ((), ())), preferred_element_type=F32
    ).astype(BF16)


def moved_rows(tile, table):
    return jnp.dot(table, tile, preferred_element_type=F32).astype(BF16)


def whole(array):
    return pl.BlockSpec(array.shape, lambda i: (0,) * array.ndim)


def one_of(array, place):
    return pl.BlockSpec((1,) + array.shape[1:], lambda i: (place,) + (0,) * (array.ndim - 1))


def scalars():
    return pl.BlockSpec(memory_space=pltpu.SMEM)


def first_kernel(
    sides_1, sides_2, inv_1, inv_2, tiles, rows, ls, lt, lc, us, ut, uc, packed, copies, forward, index
):
    solved = jnp.dot(sides_2[0], inv_2[0], preferred_element_type=F32).astype(BF16)
    forward[...] = solved
    for i in range(copies.shape[0]):
        copies[i] = solved
    blocks, extent = tiles.shape[1], tiles.shape[2]
    for b, table in enumerate(row_table(rows[0])):
        packed[b * extent : (b + 1) * extent] = moved_columns(tiles[0, b], table)
    at = blocks * extent
    packed[at : at + extent] = inv_1[0]
    at = at + extent
    packed[at : at + sides_1.shape[1]] = sides_1[0]
    at = at + sides_1.shape[1]
    for side, (source, target, count) in enumerate(((ls, lt, lc), (us, ut, uc))):
        for g in range(2):
            row = (2 * side + g) * 2 * blocks
            for b in range(blocks):
                goal = jnp.where(b < count[g], target[g, b], NOWHERE)
                index[row + b : row + b + 1] = jnp.full((1, extent), source[g, b], jnp.int32)
                index[row + blocks + b : row + blocks + b + 1] = jnp.full((1, extent), goal, jnp.int32)
    packed[at : at + index.shape[0]] = index[...].astype(F32).astype(BF16)


def later_kernel(sides_0, low_inv_0, up_inv_0, up_inv_1, low, up, low_rows, up_rows, start, packed):
    blocks, extent = low.shape[1], low.shape[2]
    for b, table in enumerate(row_table(low_rows[0])):
        packed[b * extent : (b + 1) * extent] = moved_columns(low[0, b], table)
    for g in range(2):
        for b, table in enumerate(row_table(up_rows[g])):
            at = ((1 + g) * blocks + b) * extent
            packed[at : at + extent] = moved_rows(up[g, b], table)
    at = 3 * blocks * extent
    for piece in (low_inv_0, up_inv_0, up_inv_1):
        packed[at : at + extent] = piece[0]
        at = at + extent
    packed[at : at + sides_0.shape[1]] = sides_0[0]


def swapped(value, axis):
    return lax.ppermute(value, axis, [(0, 1), (1, 0)])


def offsets():
    return [(step // 2, step % 2) for step in range(SPLIT)]


def scatter_kernel(group, level, by_target, after, place, table, column, *refs):
    tiles, before = refs[:SPLIT], refs[SPLIT] if after else None
    partial, terms, sums = (refs[-2], None, refs[-1]) if after else refs[-3:]
    zl, core = place[0], place[1]
    extent = column.shape[3]
    blocks = tiles[0].shape[0] // extent
    targets = partial.shape[1] if by_target else partial.shape[0]
    sums[...] = jnp.zeros(sums.shape, F32)

    def add(step, entry, row, term):
        goal = table[step, entry] - level * targets
        slot = jnp.where((goal >= 0) & (goal < targets), goal, targets)
        at = (pl.ds(row, 1), pl.ds(slot, 1)) if by_target else (pl.ds(slot, 1), pl.ds(row, 1))
        sums[at] = sums[at] + term[None, None]

    for step, (dz, dc) in enumerate(offsets()):
        half, row = lax.bitwise_xor(core, dc), lax.bitwise_xor(zl, dz)
        for b in range(blocks):
            source = jnp.clip(table[step, 2 * blocks * group + b], 0, column.shape[0] - 1)
            term = jnp.dot(
                column[pl.ds(source, 1), pl.ds(half, 1)][0, 0],
                tiles[step][b * extent : (b + 1) * extent],
                preferred_element_type=F32,
            )
            if not after:
                terms[step, b] = term
            add(step, 2 * blocks * group + blocks + b, row, term)
            if after:
                add(step, 2 * blocks * (group - 1) + blocks + b, row, before[step, b])
    partial[...] = (sums[:, :targets] if by_target else sums[:targets]).astype(BF16)


def full_product(operand, inverse):
    high = operand.astype(BF16)
    rest = operand - high.astype(F32)
    middle = rest.astype(BF16)
    low = (rest - middle.astype(F32)).astype(BF16)
    parts = jnp.concatenate([high, middle, low], axis=0)
    product = jnp.dot(parts, inverse, preferred_element_type=F32)
    rows = operand.shape[0]
    return product[:rows] + (product[rows : 2 * rows] + product[2 * rows :])


def solve_kernel(kind, place, got, *refs):
    inverses, refs = refs[:SPLIT], refs[SPLIT:]
    zl, core = place[0], place[1]
    rows = got.shape[3]
    me = 2 * zl + core
    if kind == 2:
        held, (solved, copies) = refs[0], refs[1:]
    elif kind == 1:
        sides, uppers, (solved, copies) = refs[:SPLIT], refs[SPLIT : 2 * SPLIT], refs[2 * SPLIT :]
    else:
        sides, (solved, copies) = refs[:SPLIT], refs[SPLIT:]
    for step, (dz, dc) in enumerate(offsets()):
        row, col = lax.bitwise_xor(zl, dz), lax.bitwise_xor(core, dc)
        total = jnp.zeros(got.shape[3:], F32)
        for i in range(got.shape[0]):
            total = total + got[i, pl.ds(col, 1), pl.ds(row, 1)][0, 0].astype(F32)
        if kind == 2:
            operand = held[step].astype(F32) - total
        else:
            mine = sides[step][pl.ds(pl.multiple_of(me * rows, rows), rows)]
            operand = mine.astype(F32) - total
        result = full_product(operand, inverses[step][...]).astype(BF16)
        if kind == 1:
            result = jnp.dot(result, uppers[step][...], preferred_element_type=F32).astype(BF16)
        solved[step] = result
        for i in range(copies.shape[0]):
            copies[i, pl.ds(row, 1), pl.ds(col, 1)] = result[None, None]


def last_kernel(place, got, forward, inverse, home_0, home_1, home_2, home_3, out):
    zl, core = place[0], place[1]
    rows = got.shape[3]
    me = 2 * zl + core
    for step, home in enumerate((home_0, home_1, home_2, home_3)):
        at = pl.multiple_of(lax.bitwise_xor(me, step) * rows, rows)
        for level in range(2):
            out[level, pl.ds(at, rows)] = home[level]
    for pair in range(got.shape[0]):
        for core_at in range(got.shape[2]):
            total = jnp.zeros(got.shape[3:], F32)
            for i in range(got.shape[1]):
                total = total + got[pair, i, core_at].astype(F32)
            at = (2 * pair + core_at) * rows
            operand = forward[at : at + rows].astype(F32) - total
            out[2, at : at + rows] = full_product(operand, inverse[0]).astype(BF16)


def row_exchange(partial):
    cores = lax.axis_size("core")
    chunks = partial.reshape((-1, cores) + partial.shape[1:])
    return lax.all_to_all(chunks, ("x", "y"), 0, 0, tiled=True)


def gather_column(copies):
    got = lax.all_to_all(copies, "zh", 0, 0, tiled=True)
    return got.reshape((-1,) + got.shape[2:])


def body(
    right_sides,
    lower_inverse,
    upper_inverse,
    lower_tiles,
    lower_source,
    lower_target,
    lower_rows,
    lower_count,
    upper_tiles,
    upper_source,
    upper_target,
    upper_rows,
    upper_count,
):
    sides = right_sides[0, 0, :, 0]
    low_inv, up_inv = lower_inverse[0, 0, :, 0], upper_inverse[0, 0, :, 0]
    low_tiles, up_tiles = lower_tiles[0, 0], upper_tiles[0, 0]
    low_rows, up_rows = lower_rows[0, 0], upper_rows[0, 0]
    low_source, low_target, low_count = lower_source[0, 0], lower_target[0, 0], lower_count[0, 0]
    up_source, up_target, up_count = upper_source[0, 0], upper_target[0, 0], upper_count[0, 0]
    side_extent, extent = sides.shape[1:]
    blocks = low_tiles.shape[1]
    pair, cores = lax.axis_size("zl"), lax.axis_size("core")
    high = lax.axis_size("zh")
    row_group = lax.axis_size("x") * lax.axis_size("y") * cores
    rows = side_extent // SPLIT
    tile_rows = blocks * extent

    first_sizes = [tile_rows, extent, side_extent, 8 * blocks]
    packed, copies, forward_2 = pl.pallas_call(
        first_kernel,
        grid=(1,),
        in_specs=[one_of(sides, 1), one_of(sides, 2), one_of(low_inv, 1), one_of(low_inv, 2)]
        + [one_of(low_tiles, 0), one_of(low_rows, 0)]
        + [scalars()] * 6,
        out_shape=[
            jax.ShapeDtypeStruct((sum(first_sizes), extent), BF16),
            jax.ShapeDtypeStruct((high, side_extent, extent), BF16),
            jax.ShapeDtypeStruct((side_extent, extent), BF16),
        ],
        out_specs=[
            pl.BlockSpec((sum(first_sizes), extent), lambda i: (0, 0)),
            pl.BlockSpec((high, side_extent, extent), lambda i: (0, 0, 0)),
            pl.BlockSpec((side_extent, extent), lambda i: (0, 0)),
        ],
        scratch_shapes=[pltpu.VMEM((8 * blocks, extent), jnp.int32)],
        compiler_params=pltpu.CompilerParams(vmem_limit_bytes=56 << 20),
    )(
        *(sides, sides, low_inv, low_inv, low_tiles, low_rows),
        *(low_source, low_target, low_count, up_source, up_target, up_count),
    )
    z_mate = swapped(packed, "zl")
    copies = copies.reshape(-1, rows, extent)
    column = lax.all_to_all(copies, ("zh", "zl", "core"), 0, 0, tiled=True)
    column = column.reshape(-1, cores, rows, extent)
    packed, z_mate = lax.optimization_barrier((packed, z_mate))
    first = (packed, swapped(packed, "core"), z_mate, swapped(z_mate, "core"))

    later_sizes = [tile_rows] * 3 + [extent] * 3 + [side_extent]
    start = first[3][:16]
    packed = pl.pallas_call(
        later_kernel,
        grid=(1,),
        in_specs=[one_of(sides, 0), one_of(low_inv, 0), one_of(up_inv, 0), one_of(up_inv, 1)]
        + [one_of(low_tiles, 1), whole(up_tiles), one_of(low_rows, 1), whole(up_rows), whole(start)],
        out_shape=jax.ShapeDtypeStruct((sum(later_sizes), extent), BF16),
        out_specs=pl.BlockSpec((sum(later_sizes), extent), lambda i: (0, 0)),
        compiler_params=pltpu.CompilerParams(vmem_limit_bytes=16 << 20),
    )(sides, low_inv, up_inv, up_inv, low_tiles, up_tiles, low_rows, up_rows, start)
    z_mate = swapped(packed, "zl")
    later = (packed, swapped(packed, "core"), z_mate, swapped(z_mate, "core"))

    place = jnp.stack([lax.axis_index("zl"), lax.axis_index("core")]).astype(jnp.int32)

    def rows_of(sizes, number):
        start, size = sum(sizes[:number]), sizes[number]
        return pl.BlockSpec((size, extent), lambda i: (start // size, 0))

    table = jnp.stack([buffer[-8 * blocks :, 0] for buffer in first])
    table = table.astype(F32).astype(jnp.int32)

    def edge(column, buffers, tile_block, group, level, before=None, by_target=False):
        shape = (row_group, pair) if not by_target else (pair, row_group)
        partial = jax.ShapeDtypeStruct(shape + (rows, extent), BF16)
        terms = jax.ShapeDtypeStruct((SPLIT, blocks, rows, extent), F32)
        extra = () if before is None else (before,)
        extra_specs = [whole(array) for array in extra]
        sums = (row_group + 1, pair) if not by_target else (pair, row_group + 1)
        return pl.pallas_call(
            functools.partial(scatter_kernel, group, level, by_target, before is not None),
            grid=(1,),
            in_specs=[scalars(), scalars(), whole(column)] + [tile_block] * SPLIT + extra_specs,
            out_shape=[partial, terms] if before is None else [partial],
            out_specs=[whole(partial), whole(terms)] if before is None else [whole(partial)],
            scratch_shapes=[pltpu.VMEM(sums + (rows, extent), F32)],
            compiler_params=pltpu.CompilerParams(vmem_limit_bytes=16 << 20),
        )(place, table, column, *buffers, *extra)

    def solve(kind, got, *pieces):
        solved = jax.ShapeDtypeStruct((SPLIT, rows, extent), BF16)
        copies = jax.ShapeDtypeStruct((high, pair, cores, rows, extent), BF16)
        arrays, specs = [], []
        for buffers, block in pieces:
            arrays += buffers
            specs += [block] * len(buffers)
        return pl.pallas_call(
            functools.partial(solve_kernel, kind),
            grid=(1,),
            in_specs=[scalars(), whole(got)] + specs,
            out_shape=[solved, copies],
            out_specs=[whole(solved), whole(copies)],
            compiler_params=pltpu.CompilerParams(vmem_limit_bytes=16 << 20),
        )(place, got, *arrays)

    partial, terms = edge(column, first, rows_of(first_sizes, 0), 0, 1)
    got = row_exchange(partial)
    inverse, side = rows_of(first_sizes, 1), rows_of(first_sizes, 2)
    forward_1, copies = solve(0, got, (first, inverse), (first, side))
    column = gather_column(copies)
    (partial,) = edge(column, later, rows_of(later_sizes, 0), 1, 0, terms)
    got = row_exchange(partial)
    inverse, upper, side = (rows_of(later_sizes, i) for i in (3, 4, 6))
    solution_0, copies = solve(1, got, (later, inverse), (later, side), (later, upper))

    column = gather_column(copies)
    partial, terms = edge(column, later, rows_of(later_sizes, 1), 2, 0)
    got = row_exchange(partial)
    solution_1, copies = solve(2, got, (later, rows_of(later_sizes, 5)), ([forward_1], whole(forward_1)))
    column = gather_column(copies)

    done = jnp.stack([solution_0, solution_1], axis=1)
    home = [done[0]]
    for step in range(1, SPLIT):
        home.append(lax.ppermute(done[step], GROUP, [(i, i ^ step) for i in range(SPLIT)]))
    column, *home = lax.optimization_barrier((column, *home))
    (partial,) = edge(column, later, rows_of(later_sizes, 2), 3, 1, terms, by_target=True)
    got = lax.all_to_all(partial.reshape(-1, rows, extent), ("zl", "x", "y", "core"), 0, 0, tiled=True)
    got = got.reshape(pair, row_group // cores, cores, rows, extent)
    result = jax.ShapeDtypeStruct(sides.shape, BF16)
    result = pl.pallas_call(
        last_kernel,
        grid=(1,),
        in_specs=[scalars(), whole(got), whole(forward_2), one_of(up_inv, 2)]
        + [whole(piece) for piece in home],
        out_shape=result,
        out_specs=whole(result),
        compiler_params=pltpu.CompilerParams(vmem_limit_bytes=16 << 20),
    )(place, got, forward_2, up_inv, *home)
    return result[None, None, :, None]


def solution(mesh):
    z_extent = mesh.shape["prow"]
    grid = mesh.devices.reshape(z_extent // 2, 2, 4, 4, 2)
    split_mesh = Mesh(grid, ("zh", "zl", "x", "y", "core"))
    row, col = ("zh", "zl"), ("x", "y", "core")
    ranks = (6, 6, 6, 6, 4, 4, 5, 3, 6, 4, 4, 5, 3)
    placed = tuple(P(row, col, *([None] * (rank - 2))) for rank in ranks)
    return jax.shard_map(
        body,
        mesh=split_mesh,
        in_specs=placed,
        out_specs=P(row, col, None, None, None, None),
        check_vma=False,
    )
```

```python
import functools

import jax
import jax.numpy as jnp
from jax import lax
from jax.experimental import pallas as pl
from jax.experimental.pallas import tpu as pltpu
from jax.sharding import Mesh
from jax.sharding import PartitionSpec as P

BF16 = jnp.bfloat16
F32 = jnp.float32
GROUP = ("zl", "core")
SPLIT = 4
NOWHERE = 255


def row_table(rows):
    places = lax.broadcasted_iota(jnp.int32, (rows.shape[-1],) * 2, 0)
    return [jnp.where(rows[b : b + 1] == places, 1.0, 0.0).astype(BF16) for b in range(rows.shape[0])]


def moved_columns(tile, table):
    return lax.dot_general(
        tile, table, (((1,), (1,)), ((), ())), preferred_element_type=F32
    ).astype(BF16)


def moved_rows(tile, table):
    return jnp.dot(table, tile, preferred_element_type=F32).astype(BF16)


def whole(array):
    return pl.BlockSpec(array.shape, lambda i: (0,) * array.ndim)


def one_of(array, place):
    return pl.BlockSpec((1,) + array.shape[1:], lambda i: (place,) + (0,) * (array.ndim - 1))


def scalars():
    return pl.BlockSpec(memory_space=pltpu.SMEM)


def first_kernel(
    sides_1, sides_2, inv_1, inv_2, tiles, rows, ls, lt, lc, us, ut, uc, packed, copies, forward, index
):
    solved = jnp.dot(sides_2[0], inv_2[0], preferred_element_type=F32).astype(BF16)
    forward[...] = solved
    for i in range(copies.shape[0]):
        copies[i] = solved
    blocks, extent = tiles.shape[1], tiles.shape[2]
    for b, table in enumerate(row_table(rows[0])):
        packed[b * extent : (b + 1) * extent] = moved_columns(tiles[0, b], table)
    at = blocks * extent
    packed[at : at + extent] = inv_1[0]
    at = at + extent
    packed[at : at + sides_1.shape[1]] = sides_1[0]
    at = at + sides_1.shape[1]
    for side, (source, target, count) in enumerate(((ls, lt, lc), (us, ut, uc))):
        for g in range(2):
            row = (2 * side + g) * 2 * blocks
            for b in range(blocks):
                goal = jnp.where(b < count[g], target[g, b], NOWHERE)
                index[row + b : row + b + 1] = jnp.full((1, extent), source[g, b], jnp.int32)
                index[row + blocks + b : row + blocks + b + 1] = jnp.full((1, extent), goal, jnp.int32)
    packed[at : at + index.shape[0]] = index[...].astype(F32).astype(BF16)


def later_kernel(sides_0, low_inv_0, up_inv_0, up_inv_1, low, up, low_rows, up_rows, start, packed):
    blocks, extent = low.shape[1], low.shape[2]
    for b, table in enumerate(row_table(low_rows[0])):
        packed[b * extent : (b + 1) * extent] = moved_columns(low[0, b], table)
    for g in range(2):
        for b, table in enumerate(row_table(up_rows[g])):
            at = ((1 + g) * blocks + b) * extent
            packed[at : at + extent] = moved_rows(up[g, b], table)
    at = 3 * blocks * extent
    for piece in (low_inv_0, up_inv_0, up_inv_1):
        packed[at : at + extent] = piece[0]
        at = at + extent
    packed[at : at + sides_0.shape[1]] = sides_0[0]


def swapped(value, axis):
    return lax.ppermute(value, axis, [(0, 1), (1, 0)])


def offsets():
    return [(step // 2, step % 2) for step in range(SPLIT)]


def scatter_kernel(group, level, by_target, after, place, table, column, *refs):
    tiles, before = refs[:SPLIT], refs[SPLIT] if after else None
    partial, terms, sums = (refs[-2], None, refs[-1]) if after else refs[-3:]
    zl, core = place[0], place[1]
    extent = column.shape[3]
    blocks = tiles[0].shape[0] // extent
    targets = partial.shape[1] if by_target else partial.shape[0]
    sums[...] = jnp.zeros(sums.shape, F32)

    def add(step, entry, row, term):
        goal = table[step, entry] - level * targets
        slot = jnp.where((goal >= 0) & (goal < targets), goal, targets)
        at = (pl.ds(row, 1), pl.ds(slot, 1)) if by_target else (pl.ds(slot, 1), pl.ds(row, 1))
        sums[at] = sums[at] + term[None, None]

    products = []
    for step, (dz, dc) in enumerate(offsets()):
        half = lax.bitwise_xor(core, dc)
        for b in range(blocks):
            source = jnp.clip(table[step, 2 * blocks * group + b], 0, column.shape[0] - 1)
            products.append(
                jnp.dot(
                    column[pl.ds(source, 1), pl.ds(half, 1)][0, 0],
                    tiles[step][b * extent : (b + 1) * extent],
                    preferred_element_type=F32,
                )
            )
    for step, (dz, dc) in enumerate(offsets()):
        row = lax.bitwise_xor(zl, dz)
        for b in range(blocks):
            if after:
                add(step, 2 * blocks * (group - 1) + blocks + b, row, before[step, b])
            else:
                terms[step, b] = products[step * blocks + b]
    for step, (dz, dc) in enumerate(offsets()):
        row = lax.bitwise_xor(zl, dz)
        for b in range(blocks):
            add(step, 2 * blocks * group + blocks + b, row, products[step * blocks + b])
    partial[...] = (sums[:, :targets] if by_target else sums[:targets]).astype(BF16)


def tree_sum(values):
    while len(values) > 1:
        pairs = [values[i] + values[i + 1] for i in range(0, len(values) - 1, 2)]
        values = pairs + values[len(values) - len(values) % 2 :]
    return values[0]


def full_product(operand, inverse):
    high = operand.astype(BF16)
    rest = operand - high.astype(F32)
    middle = rest.astype(BF16)
    low = (rest - middle.astype(F32)).astype(BF16)
    parts = jnp.concatenate([high, middle, low], axis=0)
    product = jnp.dot(parts, inverse, preferred_element_type=F32)
    rows = operand.shape[0]
    return product[:rows] + (product[rows : 2 * rows] + product[2 * rows :])


def solve_kernel(kind, got, *refs):
    inverses, refs = refs[:SPLIT], refs[SPLIT:]
    zl, core = lax.axis_index("zl"), lax.axis_index("core")
    rows = got.shape[3]
    me = 2 * zl + core
    if kind == 2:
        held, (solved, copies) = refs[0], refs[1:]
    elif kind == 1:
        sides, uppers, (solved, copies) = refs[:SPLIT], refs[SPLIT : 2 * SPLIT], refs[2 * SPLIT :]
    else:
        sides, (solved, copies) = refs[:SPLIT], refs[SPLIT:]
    places = [(lax.bitwise_xor(zl, dz), lax.bitwise_xor(core, dc)) for dz, dc in offsets()]
    operands = []
    for step, (row, col) in enumerate(places):
        pieces = [got[i, pl.ds(col, 1), pl.ds(row, 1)][0, 0].astype(F32) for i in range(got.shape[0])]
        if kind == 2:
            mine = held[step]
        else:
            mine = sides[step][pl.ds(pl.multiple_of(me * rows, rows), rows)]
        operands.append(mine.astype(F32) - tree_sum(pieces))
    results = [full_product(operands[step], inverses[step][...]) for step in range(SPLIT)]
    results = [result.astype(BF16) for result in results]
    if kind == 1:
        results = [
            jnp.dot(results[step], uppers[step][...], preferred_element_type=F32).astype(BF16)
            for step in range(SPLIT)
        ]
    for step, (row, col) in enumerate(places):
        solved[step] = results[step]
        for i in range(copies.shape[0]):
            copies[i, pl.ds(row, 1), pl.ds(col, 1)] = results[step][None, None]


def last_kernel(got, forward, inverse, home_0, home_1, home_2, home_3, out):
    zl, core = lax.axis_index("zl"), lax.axis_index("core")
    rows = got.shape[3]
    me = 2 * zl + core
    for step, home in enumerate((home_0, home_1, home_2, home_3)):
        at = pl.multiple_of(lax.bitwise_xor(me, step) * rows, rows)
        for level in range(2):
            out[level, pl.ds(at, rows)] = home[level]
    totals = [
        tree_sum([got[pair, i, col].astype(F32) for i in range(got.shape[1])])
        for pair in range(got.shape[0])
        for col in range(got.shape[2])
    ]
    operand = forward[...].astype(F32) - jnp.concatenate(totals, axis=0)
    out[2] = full_product(operand, inverse[0]).astype(BF16)


def row_exchange(partial):
    cores = lax.axis_size("core")
    chunks = partial.reshape((-1, cores) + partial.shape[1:])
    return lax.all_to_all(chunks, ("x", "y"), 0, 0, tiled=True)


def gather_column(copies):
    got = lax.all_to_all(copies, "zh", 0, 0, tiled=True)
    return got.reshape((-1,) + got.shape[2:])


def body(
    right_sides,
    lower_inverse,
    upper_inverse,
    lower_tiles,
    lower_source,
    lower_target,
    lower_rows,
    lower_count,
    upper_tiles,
    upper_source,
    upper_target,
    upper_rows,
    upper_count,
):
    sides = right_sides[0, 0, :, 0]
    low_inv, up_inv = lower_inverse[0, 0, :, 0], upper_inverse[0, 0, :, 0]
    low_tiles, up_tiles = lower_tiles[0, 0], upper_tiles[0, 0]
    low_rows, up_rows = lower_rows[0, 0], upper_rows[0, 0]
    low_source, low_target, low_count = lower_source[0, 0], lower_target[0, 0], lower_count[0, 0]
    up_source, up_target, up_count = upper_source[0, 0], upper_target[0, 0], upper_count[0, 0]
    side_extent, extent = sides.shape[1:]
    blocks = low_tiles.shape[1]
    pair, cores = lax.axis_size("zl"), lax.axis_size("core")
    high = lax.axis_size("zh")
    row_group = lax.axis_size("x") * lax.axis_size("y") * cores
    rows = side_extent // SPLIT
    tile_rows = blocks * extent

    first_sizes = [tile_rows, extent, side_extent, 8 * blocks]
    packed, copies, forward_2 = pl.pallas_call(
        first_kernel,
        grid=(1,),
        in_specs=[one_of(sides, 1), one_of(sides, 2), one_of(low_inv, 1), one_of(low_inv, 2)]
        + [one_of(low_tiles, 0), one_of(low_rows, 0)]
        + [scalars()] * 6,
        out_shape=[
            jax.ShapeDtypeStruct((sum(first_sizes), extent), BF16),
            jax.ShapeDtypeStruct((high, side_extent, extent), BF16),
            jax.ShapeDtypeStruct((side_extent, extent), BF16),
        ],
        out_specs=[
            pl.BlockSpec((sum(first_sizes), extent), lambda i: (0, 0)),
            pl.BlockSpec((high, side_extent, extent), lambda i: (0, 0, 0)),
            pl.BlockSpec((side_extent, extent), lambda i: (0, 0)),
        ],
        scratch_shapes=[pltpu.VMEM((8 * blocks, extent), jnp.int32)],
        compiler_params=pltpu.CompilerParams(vmem_limit_bytes=56 << 20),
    )(
        *(sides, sides, low_inv, low_inv, low_tiles, low_rows),
        *(low_source, low_target, low_count, up_source, up_target, up_count),
    )
    z_mate = swapped(packed, "zl")
    copies = copies.reshape(-1, rows, extent)
    column = lax.all_to_all(copies, ("zh", "zl", "core"), 0, 0, tiled=True)
    column = column.reshape(-1, cores, rows, extent)
    packed, z_mate = lax.optimization_barrier((packed, z_mate))
    first = (packed, swapped(packed, "core"), z_mate, swapped(z_mate, "core"))

    later_sizes = [tile_rows] * 3 + [extent] * 3 + [side_extent]
    start = first[3][:16]
    packed = pl.pallas_call(
        later_kernel,
        grid=(1,),
        in_specs=[one_of(sides, 0), one_of(low_inv, 0), one_of(up_inv, 0), one_of(up_inv, 1)]
        + [one_of(low_tiles, 1), whole(up_tiles), one_of(low_rows, 1), whole(up_rows), whole(start)],
        out_shape=jax.ShapeDtypeStruct((sum(later_sizes), extent), BF16),
        out_specs=pl.BlockSpec((sum(later_sizes), extent), lambda i: (0, 0)),
        compiler_params=pltpu.CompilerParams(vmem_limit_bytes=16 << 20),
    )(sides, low_inv, up_inv, up_inv, low_tiles, up_tiles, low_rows, up_rows, start)
    z_mate = swapped(packed, "zl")
    later = (packed, swapped(packed, "core"), z_mate, swapped(z_mate, "core"))

    def rows_of(sizes, number):
        start, size = sum(sizes[:number]), sizes[number]
        return pl.BlockSpec((size, extent), lambda i: (start // size, 0))

    place = jnp.stack([lax.axis_index("zl"), lax.axis_index("core")]).astype(jnp.int32)

    table = jnp.stack([buffer[-8 * blocks :, 0] for buffer in first])
    table = table.astype(F32).astype(jnp.int32)

    def edge(column, buffers, tile_block, group, level, before=None, by_target=False):
        shape = (row_group, pair) if not by_target else (pair, row_group)
        partial = jax.ShapeDtypeStruct(shape + (rows, extent), BF16)
        terms = jax.ShapeDtypeStruct((SPLIT, blocks, rows, extent), F32)
        extra = () if before is None else (before,)
        extra_specs = [whole(array) for array in extra]
        sums = (row_group + 1, pair) if not by_target else (pair, row_group + 1)
        return pl.pallas_call(
            functools.partial(scatter_kernel, group, level, by_target, before is not None),
            grid=(1,),
            in_specs=[scalars(), scalars(), whole(column)] + [tile_block] * SPLIT + extra_specs,
            out_shape=[partial, terms] if before is None else [partial],
            out_specs=[whole(partial), whole(terms)] if before is None else [whole(partial)],
            scratch_shapes=[pltpu.VMEM(sums + (rows, extent), F32)],
            compiler_params=pltpu.CompilerParams(vmem_limit_bytes=16 << 20),
        )(place, table, column, *buffers, *extra)

    def solve(kind, got, *pieces):
        solved = jax.ShapeDtypeStruct((SPLIT, rows, extent), BF16)
        copies = jax.ShapeDtypeStruct((high, pair, cores, rows, extent), BF16)
        arrays, specs = [], []
        for buffers, block in pieces:
            arrays += buffers
            specs += [block] * len(buffers)
        return pl.pallas_call(
            functools.partial(solve_kernel, kind),
            grid=(1,),
            in_specs=[whole(got)] + specs,
            out_shape=[solved, copies],
            out_specs=[whole(solved), whole(copies)],
            compiler_params=pltpu.CompilerParams(vmem_limit_bytes=16 << 20),
        )(got, *arrays)

    partial, terms = edge(column, first, rows_of(first_sizes, 0), 0, 1)
    got = row_exchange(partial)
    inverse, side = rows_of(first_sizes, 1), rows_of(first_sizes, 2)
    forward_1, copies = solve(0, got, (first, inverse), (first, side))
    column = gather_column(copies)
    (partial,) = edge(column, later, rows_of(later_sizes, 0), 1, 0, terms)
    got = row_exchange(partial)
    inverse, upper, side = (rows_of(later_sizes, i) for i in (3, 4, 6))
    solution_0, copies = solve(1, got, (later, inverse), (later, side), (later, upper))

    column = gather_column(copies)
    partial, terms = edge(column, later, rows_of(later_sizes, 1), 2, 0)
    got = row_exchange(partial)
    solution_1, copies = solve(2, got, (later, rows_of(later_sizes, 5)), ([forward_1], whole(forward_1)))
    column = gather_column(copies)

    done = jnp.stack([solution_0, solution_1], axis=1)
    home = [done[0]]
    for step in range(1, SPLIT):
        home.append(lax.ppermute(done[step], GROUP, [(i, i ^ step) for i in range(SPLIT)]))
    column, *home = lax.optimization_barrier((column, *home))
    (partial,) = edge(column, later, rows_of(later_sizes, 2), 3, 1, terms, by_target=True)
    got = lax.all_to_all(partial.reshape(-1, rows, extent), ("zl", "x", "y", "core"), 0, 0, tiled=True)
    got = got.reshape(pair, row_group // cores, cores, rows, extent)
    result = jax.ShapeDtypeStruct(sides.shape, BF16)
    result = pl.pallas_call(
        last_kernel,
        grid=(1,),
        in_specs=[whole(got), whole(forward_2), one_of(up_inv, 2)]
        + [whole(piece) for piece in home],
        out_shape=result,
        out_specs=whole(result),
        compiler_params=pltpu.CompilerParams(vmem_limit_bytes=16 << 20),
    )(got, forward_2, up_inv, *home)
    return result[None, None, :, None]


def solution(mesh):
    z_extent = mesh.shape["prow"]
    grid = mesh.devices.reshape(z_extent // 2, 2, 4, 4, 2)
    split_mesh = Mesh(grid, ("zh", "zl", "x", "y", "core"))
    row, col = ("zh", "zl"), ("x", "y", "core")
    ranks = (6, 6, 6, 6, 4, 4, 5, 3, 6, 4, 4, 5, 3)
    placed = tuple(P(row, col, *([None] * (rank - 2))) for rank in ranks)
    return jax.shard_map(
        body,
        mesh=split_mesh,
        in_specs=placed,
        out_specs=P(row, col, None, None, None, None),
        check_vma=False,
    )
```

```python
import functools

import jax
import jax.numpy as jnp
from jax import lax
from jax.experimental import pallas as pl
from jax.experimental.pallas import tpu as pltpu
from jax.sharding import Mesh
from jax.sharding import PartitionSpec as P

BF16 = jnp.bfloat16
F32 = jnp.float32
GROUP = ("zl", "core")
SPLIT = 4
NOWHERE = 255


def row_table(rows):
    places = lax.broadcasted_iota(jnp.int32, (rows.shape[-1],) * 2, 0)
    return [jnp.where(rows[b : b + 1] == places, 1.0, 0.0).astype(BF16) for b in range(rows.shape[0])]


def moved_columns(tile, table):
    return lax.dot_general(
        tile, table, (((1,), (1,)), ((), ())), preferred_element_type=F32
    ).astype(BF16)


def moved_rows(tile, table):
    return jnp.dot(table, tile, preferred_element_type=F32).astype(BF16)


def whole(array):
    return pl.BlockSpec(array.shape, lambda i: (0,) * array.ndim)


def one_of(array, place):
    return pl.BlockSpec((1,) + array.shape[1:], lambda i: (place,) + (0,) * (array.ndim - 1))


def scalars():
    return pl.BlockSpec(memory_space=pltpu.SMEM)


def first_kernel(
    sides_1, sides_2, inv_1, inv_2, tiles, rows, ls, lt, lc, us, ut, uc, packed, copies, forward, index
):
    solved = jnp.dot(sides_2[0], inv_2[0], preferred_element_type=F32).astype(BF16)
    forward[...] = solved
    for i in range(copies.shape[0]):
        copies[i] = solved
    blocks, extent = tiles.shape[1], tiles.shape[2]
    for b, table in enumerate(row_table(rows[0])):
        packed[b * extent : (b + 1) * extent] = moved_columns(tiles[0, b], table)
    at = blocks * extent
    packed[at : at + extent] = inv_1[0]
    at = at + extent
    packed[at : at + sides_1.shape[1]] = sides_1[0]
    at = at + sides_1.shape[1]
    for side, (source, target, count) in enumerate(((ls, lt, lc), (us, ut, uc))):
        for g in range(2):
            row = (2 * side + g) * 2 * blocks
            for b in range(blocks):
                goal = jnp.where(b < count[g], target[g, b], NOWHERE)
                index[row + b : row + b + 1] = jnp.full((1, extent), source[g, b], jnp.int32)
                index[row + blocks + b : row + blocks + b + 1] = jnp.full((1, extent), goal, jnp.int32)
    packed[at : at + index.shape[0]] = index[...].astype(F32).astype(BF16)


def later_kernel(sides_0, low_inv_0, up_inv_0, up_inv_1, low, up, low_rows, up_rows, start, packed):
    blocks, extent = low.shape[1], low.shape[2]
    for b, table in enumerate(row_table(low_rows[0])):
        packed[b * extent : (b + 1) * extent] = moved_columns(low[0, b], table)
    for g in range(2):
        for b, table in enumerate(row_table(up_rows[g])):
            at = ((1 + g) * blocks + b) * extent
            packed[at : at + extent] = moved_rows(up[g, b], table)
    at = 3 * blocks * extent
    for piece in (low_inv_0, up_inv_0, up_inv_1):
        packed[at : at + extent] = piece[0]
        at = at + extent
    packed[at : at + sides_0.shape[1]] = sides_0[0]


def swapped(value, axis):
    return lax.ppermute(value, axis, [(0, 1), (1, 0)])


def offsets():
    return [(step // 2, step % 2) for step in range(SPLIT)]


def scatter_kernel(group, level, by_target, after, place, table, column, *refs):
    tiles, before = refs[:SPLIT], refs[SPLIT] if after else None
    partial, terms, sums = (refs[-2], None, refs[-1]) if after else refs[-3:]
    zl, core = lax.axis_index("zl"), lax.axis_index("core")
    entries = table[...]
    extent = column.shape[3]
    blocks = tiles[0].shape[0] // extent
    targets = partial.shape[1] if by_target else partial.shape[0]
    sums[...] = jnp.zeros(sums.shape, F32)

    def add(step, entry, row, term):
        goal = entries[step, entry] - level * targets
        slot = jnp.where((goal >= 0) & (goal < targets), goal, targets)
        at = (pl.ds(row, 1), pl.ds(slot, 1)) if by_target else (pl.ds(slot, 1), pl.ds(row, 1))
        sums[at] = sums[at] + term[None, None]

    products = []
    for step, (dz, dc) in enumerate(offsets()):
        half = lax.bitwise_xor(core, dc)
        for b in range(blocks):
            source = jnp.clip(entries[step, 2 * blocks * group + b], 0, column.shape[0] - 1)
            products.append(
                jnp.dot(
                    column[pl.ds(source, 1), pl.ds(half, 1)][0, 0],
                    tiles[step][b * extent : (b + 1) * extent],
                    preferred_element_type=F32,
                )
            )
    for step, (dz, dc) in enumerate(offsets()):
        row = lax.bitwise_xor(zl, dz)
        for b in range(blocks):
            if after:
                add(step, 2 * blocks * (group - 1) + blocks + b, row, before[step, b])
            else:
                terms[step, b] = products[step * blocks + b]
    for step, (dz, dc) in enumerate(offsets()):
        row = lax.bitwise_xor(zl, dz)
        for b in range(blocks):
            add(step, 2 * blocks * group + blocks + b, row, products[step * blocks + b])
    partial[...] = (sums[:, :targets] if by_target else sums[:targets]).astype(BF16)


def tree_sum(values):
    while len(values) > 1:
        pairs = [values[i] + values[i + 1] for i in range(0, len(values) - 1, 2)]
        values = pairs + values[len(values) - len(values) % 2 :]
    return values[0]


def full_product(operand, inverse):
    high = operand.astype(BF16)
    rest = operand - high.astype(F32)
    middle = rest.astype(BF16)
    low = (rest - middle.astype(F32)).astype(BF16)
    parts = jnp.concatenate([high, middle, low], axis=0)
    product = jnp.dot(parts, inverse, preferred_element_type=F32)
    rows = operand.shape[0]
    return product[:rows] + (product[rows : 2 * rows] + product[2 * rows :])


def solve_kernel(kind, got, *refs):
    inverses, refs = refs[:SPLIT], refs[SPLIT:]
    zl, core = lax.axis_index("zl"), lax.axis_index("core")
    rows = got.shape[3]
    me = 2 * zl + core
    if kind == 2:
        held, (solved, copies) = refs[0], refs[1:]
    elif kind == 1:
        sides, uppers, (solved, copies) = refs[:SPLIT], refs[SPLIT : 2 * SPLIT], refs[2 * SPLIT :]
    else:
        sides, (solved, copies) = refs[:SPLIT], refs[SPLIT:]
    places = [(lax.bitwise_xor(zl, dz), lax.bitwise_xor(core, dc)) for dz, dc in offsets()]
    operands = []
    for step, (row, col) in enumerate(places):
        pieces = [got[i, pl.ds(col, 1), pl.ds(row, 1)][0, 0].astype(F32) for i in range(got.shape[0])]
        if kind == 2:
            mine = held[step]
        else:
            mine = sides[step][pl.ds(pl.multiple_of(me * rows, rows), rows)]
        operands.append(mine.astype(F32) - tree_sum(pieces))
    results = [full_product(operands[step], inverses[step][...]) for step in range(SPLIT)]
    results = [result.astype(BF16) for result in results]
    if kind == 1:
        results = [
            jnp.dot(results[step], uppers[step][...], preferred_element_type=F32).astype(BF16)
            for step in range(SPLIT)
        ]
    for step, (row, col) in enumerate(places):
        solved[step] = results[step]
        for i in range(copies.shape[0]):
            copies[i, pl.ds(row, 1), pl.ds(col, 1)] = results[step][None, None]


def last_kernel(got, forward, inverse, home_0, home_1, home_2, home_3, out):
    zl, core = lax.axis_index("zl"), lax.axis_index("core")
    rows = got.shape[3]
    me = 2 * zl + core
    for step, home in enumerate((home_0, home_1, home_2, home_3)):
        at = pl.multiple_of(lax.bitwise_xor(me, step) * rows, rows)
        for level in range(2):
            out[level, pl.ds(at, rows)] = home[level]
    totals = [
        tree_sum([got[pair, i, col].astype(F32) for i in range(got.shape[1])])
        for pair in range(got.shape[0])
        for col in range(got.shape[2])
    ]
    operand = forward[...].astype(F32) - jnp.concatenate(totals, axis=0)
    out[2] = full_product(operand, inverse[0]).astype(BF16)


def row_exchange(partial):
    cores = lax.axis_size("core")
    chunks = partial.reshape((-1, cores) + partial.shape[1:])
    return lax.all_to_all(chunks, ("x", "y"), 0, 0, tiled=True)


def gather_column(copies):
    got = lax.all_to_all(copies, "zh", 0, 0, tiled=True)
    return got.reshape((-1,) + got.shape[2:])


def body(
    right_sides,
    lower_inverse,
    upper_inverse,
    lower_tiles,
    lower_source,
    lower_target,
    lower_rows,
    lower_count,
    upper_tiles,
    upper_source,
    upper_target,
    upper_rows,
    upper_count,
):
    sides = right_sides[0, 0, :, 0]
    low_inv, up_inv = lower_inverse[0, 0, :, 0], upper_inverse[0, 0, :, 0]
    low_tiles, up_tiles = lower_tiles[0, 0], upper_tiles[0, 0]
    low_rows, up_rows = lower_rows[0, 0], upper_rows[0, 0]
    low_source, low_target, low_count = lower_source[0, 0], lower_target[0, 0], lower_count[0, 0]
    up_source, up_target, up_count = upper_source[0, 0], upper_target[0, 0], upper_count[0, 0]
    side_extent, extent = sides.shape[1:]
    blocks = low_tiles.shape[1]
    pair, cores = lax.axis_size("zl"), lax.axis_size("core")
    high = lax.axis_size("zh")
    row_group = lax.axis_size("x") * lax.axis_size("y") * cores
    rows = side_extent // SPLIT
    tile_rows = blocks * extent

    first_sizes = [tile_rows, extent, side_extent, 8 * blocks]
    packed, copies, forward_2 = pl.pallas_call(
        first_kernel,
        grid=(1,),
        in_specs=[one_of(sides, 1), one_of(sides, 2), one_of(low_inv, 1), one_of(low_inv, 2)]
        + [one_of(low_tiles, 0), one_of(low_rows, 0)]
        + [scalars()] * 6,
        out_shape=[
            jax.ShapeDtypeStruct((sum(first_sizes), extent), BF16),
            jax.ShapeDtypeStruct((high, side_extent, extent), BF16),
            jax.ShapeDtypeStruct((side_extent, extent), BF16),
        ],
        out_specs=[
            pl.BlockSpec((sum(first_sizes), extent), lambda i: (0, 0)),
            pl.BlockSpec((high, side_extent, extent), lambda i: (0, 0, 0)),
            pl.BlockSpec((side_extent, extent), lambda i: (0, 0)),
        ],
        scratch_shapes=[pltpu.VMEM((8 * blocks, extent), jnp.int32)],
        compiler_params=pltpu.CompilerParams(vmem_limit_bytes=56 << 20),
    )(
        *(sides, sides, low_inv, low_inv, low_tiles, low_rows),
        *(low_source, low_target, low_count, up_source, up_target, up_count),
    )
    z_mate = swapped(packed, "zl")
    copies = copies.reshape(-1, rows, extent)
    column = lax.all_to_all(copies, ("zh", "zl", "core"), 0, 0, tiled=True)
    column = column.reshape(-1, cores, rows, extent)
    packed, z_mate = lax.optimization_barrier((packed, z_mate))
    first = (packed, swapped(packed, "core"), z_mate, swapped(z_mate, "core"))

    later_sizes = [tile_rows] * 3 + [extent] * 3 + [side_extent]
    start = first[3][:16]
    packed = pl.pallas_call(
        later_kernel,
        grid=(1,),
        in_specs=[one_of(sides, 0), one_of(low_inv, 0), one_of(up_inv, 0), one_of(up_inv, 1)]
        + [one_of(low_tiles, 1), whole(up_tiles), one_of(low_rows, 1), whole(up_rows), whole(start)],
        out_shape=jax.ShapeDtypeStruct((sum(later_sizes), extent), BF16),
        out_specs=pl.BlockSpec((sum(later_sizes), extent), lambda i: (0, 0)),
        compiler_params=pltpu.CompilerParams(vmem_limit_bytes=16 << 20),
    )(sides, low_inv, up_inv, up_inv, low_tiles, up_tiles, low_rows, up_rows, start)
    z_mate = swapped(packed, "zl")
    later = (packed, swapped(packed, "core"), z_mate, swapped(z_mate, "core"))

    def rows_of(sizes, number):
        start, size = sum(sizes[:number]), sizes[number]
        return pl.BlockSpec((size, extent), lambda i: (start // size, 0))

    place = jnp.stack([lax.axis_index("zl"), lax.axis_index("core")]).astype(jnp.int32)

    table = jnp.stack([buffer[-8 * blocks :, 0] for buffer in first])
    table = table.astype(F32).astype(jnp.int32)

    def edge(column, buffers, tile_block, group, level, before=None, by_target=False):
        shape = (row_group, pair) if not by_target else (pair, row_group)
        partial = jax.ShapeDtypeStruct(shape + (rows, extent), BF16)
        terms = jax.ShapeDtypeStruct((SPLIT, blocks, rows, extent), F32)
        extra = () if before is None else (before,)
        extra_specs = [whole(array) for array in extra]
        sums = (row_group + 1, pair) if not by_target else (pair, row_group + 1)
        return pl.pallas_call(
            functools.partial(scatter_kernel, group, level, by_target, before is not None),
            grid=(1,),
            in_specs=[whole(place), whole(table), whole(column)] + [tile_block] * SPLIT + extra_specs,
            out_shape=[partial, terms] if before is None else [partial],
            out_specs=[whole(partial), whole(terms)] if before is None else [whole(partial)],
            scratch_shapes=[pltpu.VMEM(sums + (rows, extent), F32)],
            compiler_params=pltpu.CompilerParams(vmem_limit_bytes=16 << 20),
        )(place, table, column, *buffers, *extra)

    def solve(kind, got, *pieces):
        solved = jax.ShapeDtypeStruct((SPLIT, rows, extent), BF16)
        copies = jax.ShapeDtypeStruct((high, pair, cores, rows, extent), BF16)
        arrays, specs = [], []
        for buffers, block in pieces:
            arrays += buffers
            specs += [block] * len(buffers)
        return pl.pallas_call(
            functools.partial(solve_kernel, kind),
            grid=(1,),
            in_specs=[whole(got)] + specs,
            out_shape=[solved, copies],
            out_specs=[whole(solved), whole(copies)],
            compiler_params=pltpu.CompilerParams(vmem_limit_bytes=16 << 20),
        )(got, *arrays)

    partial, terms = edge(column, first, rows_of(first_sizes, 0), 0, 1)
    got = row_exchange(partial)
    inverse, side = rows_of(first_sizes, 1), rows_of(first_sizes, 2)
    forward_1, copies = solve(0, got, (first, inverse), (first, side))
    column = gather_column(copies)
    (partial,) = edge(column, later, rows_of(later_sizes, 0), 1, 0, terms)
    got = row_exchange(partial)
    inverse, upper, side = (rows_of(later_sizes, i) for i in (3, 4, 6))
    solution_0, copies = solve(1, got, (later, inverse), (later, side), (later, upper))

    column = gather_column(copies)
    partial, terms = edge(column, later, rows_of(later_sizes, 1), 2, 0)
    got = row_exchange(partial)
    solution_1, copies = solve(2, got, (later, rows_of(later_sizes, 5)), ([forward_1], whole(forward_1)))
    column = gather_column(copies)

    done = jnp.stack([solution_0, solution_1], axis=1)
    home = [done[0]]
    for step in range(1, SPLIT):
        home.append(lax.ppermute(done[step], GROUP, [(i, i ^ step) for i in range(SPLIT)]))
    column, *home = lax.optimization_barrier((column, *home))
    (partial,) = edge(column, later, rows_of(later_sizes, 2), 3, 1, terms, by_target=True)
    got = lax.all_to_all(partial.reshape(-1, rows, extent), ("zl", "x", "y", "core"), 0, 0, tiled=True)
    got = got.reshape(pair, row_group // cores, cores, rows, extent)
    result = jax.ShapeDtypeStruct(sides.shape, BF16)
    result = pl.pallas_call(
        last_kernel,
        grid=(1,),
        in_specs=[whole(got), whole(forward_2), one_of(up_inv, 2)]
        + [whole(piece) for piece in home],
        out_shape=result,
        out_specs=whole(result),
        compiler_params=pltpu.CompilerParams(vmem_limit_bytes=16 << 20),
    )(got, forward_2, up_inv, *home)
    return result[None, None, :, None]


def solution(mesh):
    z_extent = mesh.shape["prow"]
    grid = mesh.devices.reshape(z_extent // 2, 2, 4, 4, 2)
    split_mesh = Mesh(grid, ("zh", "zl", "x", "y", "core"))
    row, col = ("zh", "zl"), ("x", "y", "core")
    ranks = (6, 6, 6, 6, 4, 4, 5, 3, 6, 4, 4, 5, 3)
    placed = tuple(P(row, col, *([None] * (rank - 2))) for rank in ranks)
    return jax.shard_map(
        body,
        mesh=split_mesh,
        in_specs=placed,
        out_specs=P(row, col, None, None, None, None),
        check_vma=False,
    )
```

```python
import functools

import jax
import jax.numpy as jnp
from jax import lax
from jax.experimental import pallas as pl
from jax.experimental.pallas import tpu as pltpu
from jax.sharding import Mesh
from jax.sharding import PartitionSpec as P

BF16 = jnp.bfloat16
F32 = jnp.float32
GROUP = ("zl", "core")
SPLIT = 4
NOWHERE = 255


def row_table(rows):
    places = lax.broadcasted_iota(jnp.int32, (rows.shape[-1],) * 2, 0)
    return [jnp.where(rows[b : b + 1] == places, 1.0, 0.0).astype(BF16) for b in range(rows.shape[0])]


def moved_columns(tile, table):
    return lax.dot_general(
        tile, table, (((1,), (1,)), ((), ())), preferred_element_type=F32
    ).astype(BF16)


def moved_rows(tile, table):
    return jnp.dot(table, tile, preferred_element_type=F32).astype(BF16)


def whole(array):
    return pl.BlockSpec(array.shape, lambda i: (0,) * array.ndim)


def one_of(array, place):
    return pl.BlockSpec((1,) + array.shape[1:], lambda i: (place,) + (0,) * (array.ndim - 1))


def scalars():
    return pl.BlockSpec(memory_space=pltpu.SMEM)


def first_kernel(
    sides_1, sides_2, inv_1, inv_2, tiles, rows, ls, lt, lc, us, ut, uc, packed, copies, forward, index
):
    solved = jnp.dot(sides_2[0], inv_2[0], preferred_element_type=F32).astype(BF16)
    forward[...] = solved
    for i in range(copies.shape[0]):
        copies[i] = solved
    blocks, extent = tiles.shape[1], tiles.shape[2]
    for b, table in enumerate(row_table(rows[0])):
        packed[b * extent : (b + 1) * extent] = moved_columns(tiles[0, b], table)
    at = blocks * extent
    packed[at : at + extent] = inv_1[0]
    at = at + extent
    packed[at : at + sides_1.shape[1]] = sides_1[0]
    at = at + sides_1.shape[1]
    for side, (source, target, count) in enumerate(((ls, lt, lc), (us, ut, uc))):
        for g in range(2):
            row = (2 * side + g) * 2 * blocks
            for b in range(blocks):
                goal = jnp.where(b < count[g], target[g, b], NOWHERE)
                index[row + b : row + b + 1] = jnp.full((1, extent), source[g, b], jnp.int32)
                index[row + blocks + b : row + blocks + b + 1] = jnp.full((1, extent), goal, jnp.int32)
    packed[at : at + index.shape[0]] = index[...].astype(F32).astype(BF16)


def later_kernel(sides_0, low_inv_0, up_inv_0, up_inv_1, low, up, low_rows, up_rows, start, packed):
    blocks, extent = low.shape[1], low.shape[2]
    for b, table in enumerate(row_table(low_rows[0])):
        packed[b * extent : (b + 1) * extent] = moved_columns(low[0, b], table)
    for g in range(2):
        for b, table in enumerate(row_table(up_rows[g])):
            at = ((1 + g) * blocks + b) * extent
            packed[at : at + extent] = moved_rows(up[g, b], table)
    at = 3 * blocks * extent
    for piece in (low_inv_0, up_inv_0, up_inv_1):
        packed[at : at + extent] = piece[0]
        at = at + extent
    packed[at : at + sides_0.shape[1]] = sides_0[0]


def swapped(value, axis):
    return lax.ppermute(value, axis, [(0, 1), (1, 0)])


def offsets():
    return [(step // 2, step % 2) for step in range(SPLIT)]


def scatter_kernel(group, level, by_target, after, place, table, column, *refs):
    tiles, before = refs[:SPLIT], refs[SPLIT] if after else None
    partial, terms, sums = (refs[-2], None, refs[-1]) if after else refs[-3:]
    zl, core = lax.axis_index("zl"), lax.axis_index("core")
    entries = table[...]
    extent = column.shape[3]
    blocks = tiles[0].shape[0] // extent
    targets = partial.shape[1] if by_target else partial.shape[0]
    sums[...] = jnp.zeros(sums.shape, F32)

    def add(step, entry, row, term):
        goal = entries[step, entry] - level * targets
        slot = jnp.where((goal >= 0) & (goal < targets), goal, targets)
        at = (pl.ds(row, 1), pl.ds(slot, 1)) if by_target else (pl.ds(slot, 1), pl.ds(row, 1))
        sums[at] = sums[at] + term[None, None]

    products = []
    for step, (dz, dc) in enumerate(offsets()):
        half = lax.bitwise_xor(core, dc)
        for b in range(blocks):
            source = jnp.clip(entries[step, 2 * blocks * group + b], 0, column.shape[0] - 1)
            products.append(
                jnp.dot(
                    column[pl.ds(source, 1), pl.ds(half, 1)][0, 0],
                    tiles[step][b * extent : (b + 1) * extent],
                    preferred_element_type=F32,
                )
            )
    for step, (dz, dc) in enumerate(offsets()):
        row = lax.bitwise_xor(zl, dz)
        for b in range(blocks):
            if after:
                add(step, 2 * blocks * (group - 1) + blocks + b, row, before[step, b])
            else:
                terms[step, b] = products[step * blocks + b]
    for step, (dz, dc) in enumerate(offsets()):
        row = lax.bitwise_xor(zl, dz)
        for b in range(blocks):
            add(step, 2 * blocks * group + blocks + b, row, products[step * blocks + b])
    partial[...] = (sums[:, :targets] if by_target else sums[:targets]).astype(BF16)


def tree_sum(values):
    while len(values) > 1:
        pairs = [values[i] + values[i + 1] for i in range(0, len(values) - 1, 2)]
        values = pairs + values[len(values) - len(values) % 2 :]
    return values[0]


def full_product(operand, inverse):
    high = operand.astype(BF16)
    rest = operand - high.astype(F32)
    middle = rest.astype(BF16)
    low = (rest - middle.astype(F32)).astype(BF16)
    parts = jnp.concatenate([high, middle, low], axis=0)
    product = jnp.dot(parts, inverse, preferred_element_type=F32)
    rows = operand.shape[0]
    return product[:rows] + (product[rows : 2 * rows] + product[2 * rows :])


def solve_kernel(kind, got, *refs):
    inverses, refs = refs[:SPLIT], refs[SPLIT:]
    zl, core = lax.axis_index("zl"), lax.axis_index("core")
    rows = got.shape[3]
    me = 2 * zl + core
    if kind == 2:
        held, (solved, copies) = refs[0], refs[1:]
    elif kind == 1:
        sides, uppers, (solved, copies) = refs[:SPLIT], refs[SPLIT : 2 * SPLIT], refs[2 * SPLIT :]
    else:
        sides, (solved, copies) = refs[:SPLIT], refs[SPLIT:]
    places = [(lax.bitwise_xor(zl, dz), lax.bitwise_xor(core, dc)) for dz, dc in offsets()]
    operands = []
    for step, (row, col) in enumerate(places):
        pieces = [got[i, pl.ds(col, 1), pl.ds(row, 1)][0, 0].astype(F32) for i in range(got.shape[0])]
        if kind == 2:
            mine = held[step]
        else:
            mine = sides[step][pl.ds(pl.multiple_of(me * rows, rows), rows)]
        operands.append(mine.astype(F32) - tree_sum(pieces))
    results = [full_product(operands[step], inverses[step][...]) for step in range(SPLIT)]
    results = [result.astype(BF16) for result in results]
    if kind == 1:
        results = [
            jnp.dot(results[step], uppers[step][...], preferred_element_type=F32).astype(BF16)
            for step in range(SPLIT)
        ]
    for step, (row, col) in enumerate(places):
        solved[step] = results[step]
        for i in range(copies.shape[0]):
            copies[i, pl.ds(row, 1), pl.ds(col, 1)] = results[step][None, None]


def last_kernel(got, forward, inverse, home_0, home_1, home_2, home_3, out):
    zl, core = lax.axis_index("zl"), lax.axis_index("core")
    rows = got.shape[3]
    me = 2 * zl + core
    for step, home in enumerate((home_0, home_1, home_2, home_3)):
        at = pl.multiple_of(lax.bitwise_xor(me, step) * rows, rows)
        for level in range(2):
            out[level, pl.ds(at, rows)] = home[level]
    totals = [
        tree_sum([got[pair, i, col].astype(F32) for i in range(got.shape[1])])
        for pair in range(got.shape[0])
        for col in range(got.shape[2])
    ]
    operand = forward[...].astype(F32) - jnp.concatenate(totals, axis=0)
    out[2] = full_product(operand, inverse[0]).astype(BF16)


def row_exchange(partial):
    cores = lax.axis_size("core")
    chunks = partial.reshape((-1, cores) + partial.shape[1:])
    return lax.all_to_all(chunks, ("x", "y"), 0, 0, tiled=True)


def gather_column(copies):
    got = lax.all_to_all(copies, "zh", 0, 0, tiled=True)
    return got.reshape((-1,) + got.shape[2:])


def body(
    right_sides,
    lower_inverse,
    upper_inverse,
    lower_tiles,
    lower_source,
    lower_target,
    lower_rows,
    lower_count,
    upper_tiles,
    upper_source,
    upper_target,
    upper_rows,
    upper_count,
):
    sides = right_sides[0, 0, :, 0]
    low_inv, up_inv = lower_inverse[0, 0, :, 0], upper_inverse[0, 0, :, 0]
    low_tiles, up_tiles = lower_tiles[0, 0], upper_tiles[0, 0]
    low_rows, up_rows = lower_rows[0, 0], upper_rows[0, 0]
    low_source, low_target, low_count = lower_source[0, 0], lower_target[0, 0], lower_count[0, 0]
    up_source, up_target, up_count = upper_source[0, 0], upper_target[0, 0], upper_count[0, 0]
    side_extent, extent = sides.shape[1:]
    blocks = low_tiles.shape[1]
    pair, cores = lax.axis_size("zl"), lax.axis_size("core")
    high = lax.axis_size("zh")
    row_group = lax.axis_size("x") * lax.axis_size("y") * cores
    rows = side_extent // SPLIT
    tile_rows = blocks * extent

    first_sizes = [tile_rows, extent, side_extent, 8 * blocks]
    packed, copies, forward_2 = pl.pallas_call(
        first_kernel,
        grid=(1,),
        in_specs=[one_of(sides, 1), one_of(sides, 2), one_of(low_inv, 1), one_of(low_inv, 2)]
        + [one_of(low_tiles, 0), one_of(low_rows, 0)]
        + [scalars()] * 6,
        out_shape=[
            jax.ShapeDtypeStruct((sum(first_sizes), extent), BF16),
            jax.ShapeDtypeStruct((high, side_extent, extent), BF16),
            jax.ShapeDtypeStruct((side_extent, extent), BF16),
        ],
        out_specs=[
            pl.BlockSpec((sum(first_sizes), extent), lambda i: (0, 0)),
            pl.BlockSpec((high, side_extent, extent), lambda i: (0, 0, 0)),
            pl.BlockSpec((side_extent, extent), lambda i: (0, 0)),
        ],
        scratch_shapes=[pltpu.VMEM((8 * blocks, extent), jnp.int32)],
        compiler_params=pltpu.CompilerParams(vmem_limit_bytes=56 << 20),
    )(
        *(sides, sides, low_inv, low_inv, low_tiles, low_rows),
        *(low_source, low_target, low_count, up_source, up_target, up_count),
    )
    z_mate = swapped(packed, "zl")
    copies = copies.reshape(-1, rows, extent)
    column = lax.all_to_all(copies, ("zh", "zl", "core"), 0, 0, tiled=True)
    column = column.reshape(-1, cores, rows, extent)
    packed, z_mate = lax.optimization_barrier((packed, z_mate))
    first = (packed, swapped(packed, "core"), z_mate, swapped(z_mate, "core"))

    later_sizes = [tile_rows] * 3 + [extent] * 3 + [side_extent]
    start = z_mate[:16]
    packed = pl.pallas_call(
        later_kernel,
        grid=(1,),
        in_specs=[one_of(sides, 0), one_of(low_inv, 0), one_of(up_inv, 0), one_of(up_inv, 1)]
        + [one_of(low_tiles, 1), whole(up_tiles), one_of(low_rows, 1), whole(up_rows), whole(start)],
        out_shape=jax.ShapeDtypeStruct((sum(later_sizes), extent), BF16),
        out_specs=pl.BlockSpec((sum(later_sizes), extent), lambda i: (0, 0)),
        compiler_params=pltpu.CompilerParams(vmem_limit_bytes=16 << 20),
    )(sides, low_inv, up_inv, up_inv, low_tiles, up_tiles, low_rows, up_rows, start)
    z_mate = swapped(packed, "zl")
    later = (packed, swapped(packed, "core"), z_mate, swapped(z_mate, "core"))

    def rows_of(sizes, number):
        start, size = sum(sizes[:number]), sizes[number]
        return pl.BlockSpec((size, extent), lambda i: (start // size, 0))

    place = jnp.stack([lax.axis_index("zl"), lax.axis_index("core")]).astype(jnp.int32)

    table = jnp.stack([buffer[-8 * blocks :, 0] for buffer in first])
    table = table.astype(F32).astype(jnp.int32)

    def edge(column, buffers, tile_block, group, level, before=None, by_target=False):
        shape = (row_group, pair) if not by_target else (pair, row_group)
        partial = jax.ShapeDtypeStruct(shape + (rows, extent), BF16)
        terms = jax.ShapeDtypeStruct((SPLIT, blocks, rows, extent), F32)
        extra = () if before is None else (before,)
        extra_specs = [whole(array) for array in extra]
        sums = (row_group + 1, pair) if not by_target else (pair, row_group + 1)
        return pl.pallas_call(
            functools.partial(scatter_kernel, group, level, by_target, before is not None),
            grid=(1,),
            in_specs=[whole(place), whole(table), whole(column)] + [tile_block] * SPLIT + extra_specs,
            out_shape=[partial, terms] if before is None else [partial],
            out_specs=[whole(partial), whole(terms)] if before is None else [whole(partial)],
            scratch_shapes=[pltpu.VMEM(sums + (rows, extent), F32)],
            compiler_params=pltpu.CompilerParams(vmem_limit_bytes=16 << 20),
        )(place, table, column, *buffers, *extra)

    def solve(kind, got, *pieces):
        solved = jax.ShapeDtypeStruct((SPLIT, rows, extent), BF16)
        copies = jax.ShapeDtypeStruct((high, pair, cores, rows, extent), BF16)
        arrays, specs = [], []
        for buffers, block in pieces:
            arrays += buffers
            specs += [block] * len(buffers)
        return pl.pallas_call(
            functools.partial(solve_kernel, kind),
            grid=(1,),
            in_specs=[whole(got)] + specs,
            out_shape=[solved, copies],
            out_specs=[whole(solved), whole(copies)],
            compiler_params=pltpu.CompilerParams(vmem_limit_bytes=16 << 20),
        )(got, *arrays)

    partial, terms = edge(column, first, rows_of(first_sizes, 0), 0, 1)
    got = row_exchange(partial)
    inverse, side = rows_of(first_sizes, 1), rows_of(first_sizes, 2)
    forward_1, copies = solve(0, got, (first, inverse), (first, side))
    column = gather_column(copies)
    (partial,) = edge(column, later, rows_of(later_sizes, 0), 1, 0, terms)
    got = row_exchange(partial)
    inverse, upper, side = (rows_of(later_sizes, i) for i in (3, 4, 6))
    solution_0, copies = solve(1, got, (later, inverse), (later, side), (later, upper))

    column = gather_column(copies)
    partial, terms = edge(column, later, rows_of(later_sizes, 1), 2, 0)
    got = row_exchange(partial)
    solution_1, copies = solve(2, got, (later, rows_of(later_sizes, 5)), ([forward_1], whole(forward_1)))
    column = gather_column(copies)

    done = jnp.stack([solution_0, solution_1], axis=1)
    home = [done[0]]
    for step in range(1, SPLIT):
        home.append(lax.ppermute(done[step], GROUP, [(i, i ^ step) for i in range(SPLIT)]))
    column, *home = lax.optimization_barrier((column, *home))
    (partial,) = edge(column, later, rows_of(later_sizes, 2), 3, 1, terms, by_target=True)
    got = lax.all_to_all(partial.reshape(-1, rows, extent), ("zl", "x", "y", "core"), 0, 0, tiled=True)
    got = got.reshape(pair, row_group // cores, cores, rows, extent)
    result = jax.ShapeDtypeStruct(sides.shape, BF16)
    result = pl.pallas_call(
        last_kernel,
        grid=(1,),
        in_specs=[whole(got), whole(forward_2), one_of(up_inv, 2)]
        + [whole(piece) for piece in home],
        out_shape=result,
        out_specs=whole(result),
        compiler_params=pltpu.CompilerParams(vmem_limit_bytes=16 << 20),
    )(got, forward_2, up_inv, *home)
    return result[None, None, :, None]


def solution(mesh):
    z_extent = mesh.shape["prow"]
    grid = mesh.devices.reshape(z_extent // 2, 2, 4, 4, 2)
    split_mesh = Mesh(grid, ("zh", "zl", "x", "y", "core"))
    row, col = ("zh", "zl"), ("x", "y", "core")
    ranks = (6, 6, 6, 6, 4, 4, 5, 3, 6, 4, 4, 5, 3)
    placed = tuple(P(row, col, *([None] * (rank - 2))) for rank in ranks)
    return jax.shard_map(
        body,
        mesh=split_mesh,
        in_specs=placed,
        out_specs=P(row, col, None, None, None, None),
        check_vma=False,
    )
```

```python
import functools

import jax
import jax.numpy as jnp
from jax import lax
from jax.experimental import pallas as pl
from jax.experimental.pallas import tpu as pltpu
from jax.sharding import Mesh
from jax.sharding import PartitionSpec as P

BF16 = jnp.bfloat16
F32 = jnp.float32
GROUP = ("zl", "core")
SPLIT = 4
NOWHERE = 255


def row_table(rows):
    places = lax.broadcasted_iota(jnp.int32, (rows.shape[-1],) * 2, 0)
    return [jnp.where(rows[b : b + 1] == places, 1.0, 0.0).astype(BF16) for b in range(rows.shape[0])]


def moved_columns(tile, table):
    return lax.dot_general(
        tile, table, (((1,), (1,)), ((), ())), preferred_element_type=F32
    ).astype(BF16)


def moved_rows(tile, table):
    return jnp.dot(table, tile, preferred_element_type=F32).astype(BF16)


def whole(array):
    return pl.BlockSpec(array.shape, lambda i: (0,) * array.ndim)


def one_of(array, place):
    return pl.BlockSpec((1,) + array.shape[1:], lambda i: (place,) + (0,) * (array.ndim - 1))


def scalars():
    return pl.BlockSpec(memory_space=pltpu.SMEM)


def first_kernel(
    sides_1, sides_2, inv_1, inv_2, tiles, rows, ls, lt, lc, us, ut, uc, packed, copies, forward, index
):
    solved = jnp.dot(sides_2[0], inv_2[0], preferred_element_type=F32).astype(BF16)
    forward[...] = solved
    for i in range(copies.shape[0]):
        copies[i] = solved
    blocks, extent = tiles.shape[1], tiles.shape[2]
    for b, table in enumerate(row_table(rows[0])):
        packed[b * extent : (b + 1) * extent] = moved_columns(tiles[0, b], table)
    at = blocks * extent
    packed[at : at + extent] = inv_1[0]
    at = at + extent
    packed[at : at + sides_1.shape[1]] = sides_1[0]
    at = at + sides_1.shape[1]
    for side, refs in enumerate(((ls, lt, lc), (us, ut, uc))):
        source, target, count = (ref[...] for ref in refs)
        for g in range(2):
            row = (2 * side + g) * 2 * blocks
            for b in range(blocks):
                goal = jnp.where(b < count[0, g], target[g, b], NOWHERE)
                index[row + b : row + b + 1] = jnp.full((1, extent), source[g, b], jnp.int32)
                index[row + blocks + b : row + blocks + b + 1] = jnp.full((1, extent), goal, jnp.int32)
    packed[at : at + index.shape[0]] = index[...].astype(F32).astype(BF16)


def later_kernel(sides_0, low_inv_0, up_inv_0, up_inv_1, low, up, low_rows, up_rows, start, packed):
    blocks, extent = low.shape[1], low.shape[2]
    for b, table in enumerate(row_table(low_rows[0])):
        packed[b * extent : (b + 1) * extent] = moved_columns(low[0, b], table)
    for g in range(2):
        for b, table in enumerate(row_table(up_rows[g])):
            at = ((1 + g) * blocks + b) * extent
            packed[at : at + extent] = moved_rows(up[g, b], table)
    at = 3 * blocks * extent
    for piece in (low_inv_0, up_inv_0, up_inv_1):
        packed[at : at + extent] = piece[0]
        at = at + extent
    packed[at : at + sides_0.shape[1]] = sides_0[0]


def swapped(value, axis):
    return lax.ppermute(value, axis, [(0, 1), (1, 0)])


def offsets():
    return [(step // 2, step % 2) for step in range(SPLIT)]


def scatter_kernel(group, level, by_target, after, place, table, column, *refs):
    tiles, before = refs[:SPLIT], refs[SPLIT] if after else None
    partial, terms, sums = (refs[-2], None, refs[-1]) if after else refs[-3:]
    zl, core = lax.axis_index("zl"), lax.axis_index("core")
    entries = table[...]
    extent = column.shape[3]
    blocks = tiles[0].shape[0] // extent
    targets = partial.shape[1] if by_target else partial.shape[0]
    sums[...] = jnp.zeros(sums.shape, F32)

    def add(step, entry, row, term):
        goal = entries[step, entry] - level * targets
        slot = jnp.where((goal >= 0) & (goal < targets), goal, targets)
        at = (pl.ds(row, 1), pl.ds(slot, 1)) if by_target else (pl.ds(slot, 1), pl.ds(row, 1))
        sums[at] = sums[at] + term[None, None]

    products = []
    for step, (dz, dc) in enumerate(offsets()):
        half = lax.bitwise_xor(core, dc)
        for b in range(blocks):
            source = jnp.clip(entries[step, 2 * blocks * group + b], 0, column.shape[0] - 1)
            products.append(
                jnp.dot(
                    column[pl.ds(source, 1), pl.ds(half, 1)][0, 0],
                    tiles[step][b * extent : (b + 1) * extent],
                    preferred_element_type=F32,
                )
            )
    for step, (dz, dc) in enumerate(offsets()):
        row = lax.bitwise_xor(zl, dz)
        for b in range(blocks):
            if after:
                add(step, 2 * blocks * (group - 1) + blocks + b, row, before[step, b])
            else:
                terms[step, b] = products[step * blocks + b]
    for step, (dz, dc) in enumerate(offsets()):
        row = lax.bitwise_xor(zl, dz)
        for b in range(blocks):
            add(step, 2 * blocks * group + blocks + b, row, products[step * blocks + b])
    partial[...] = (sums[:, :targets] if by_target else sums[:targets]).astype(BF16)


def tree_sum(values):
    while len(values) > 1:
        pairs = [values[i] + values[i + 1] for i in range(0, len(values) - 1, 2)]
        values = pairs + values[len(values) - len(values) % 2 :]
    return values[0]


def full_product(operand, inverse):
    high = operand.astype(BF16)
    rest = operand - high.astype(F32)
    middle = rest.astype(BF16)
    low = (rest - middle.astype(F32)).astype(BF16)
    parts = jnp.concatenate([high, middle, low], axis=0)
    product = jnp.dot(parts, inverse, preferred_element_type=F32)
    rows = operand.shape[0]
    return product[:rows] + (product[rows : 2 * rows] + product[2 * rows :])


def solve_kernel(kind, got, *refs):
    inverses, refs = refs[:SPLIT], refs[SPLIT:]
    zl, core = lax.axis_index("zl"), lax.axis_index("core")
    rows = got.shape[3]
    me = 2 * zl + core
    if kind == 2:
        held, (solved, copies) = refs[0], refs[1:]
    elif kind == 1:
        sides, uppers, (solved, copies) = refs[:SPLIT], refs[SPLIT : 2 * SPLIT], refs[2 * SPLIT :]
    else:
        sides, (solved, copies) = refs[:SPLIT], refs[SPLIT:]
    places = [(lax.bitwise_xor(zl, dz), lax.bitwise_xor(core, dc)) for dz, dc in offsets()]
    operands = []
    for step, (row, col) in enumerate(places):
        pieces = [got[i, pl.ds(col, 1), pl.ds(row, 1)][0, 0].astype(F32) for i in range(got.shape[0])]
        if kind == 2:
            mine = held[step]
        else:
            mine = sides[step][pl.ds(pl.multiple_of(me * rows, rows), rows)]
        operands.append(mine.astype(F32) - tree_sum(pieces))
    results = [full_product(operands[step], inverses[step][...]) for step in range(SPLIT)]
    results = [result.astype(BF16) for result in results]
    if kind == 1:
        results = [
            jnp.dot(results[step], uppers[step][...], preferred_element_type=F32).astype(BF16)
            for step in range(SPLIT)
        ]
    for step, (row, col) in enumerate(places):
        solved[step] = results[step]
        for i in range(copies.shape[0]):
            copies[i, pl.ds(row, 1), pl.ds(col, 1)] = results[step][None, None]


def last_kernel(got, forward, inverse, home_0, home_1, home_2, home_3, out):
    zl, core = lax.axis_index("zl"), lax.axis_index("core")
    rows = got.shape[3]
    me = 2 * zl + core
    for step, home in enumerate((home_0, home_1, home_2, home_3)):
        at = pl.multiple_of(lax.bitwise_xor(me, step) * rows, rows)
        for level in range(2):
            out[level, pl.ds(at, rows)] = home[level]
    totals = [
        tree_sum([got[pair, i, col].astype(F32) for i in range(got.shape[1])])
        for pair in range(got.shape[0])
        for col in range(got.shape[2])
    ]
    operand = forward[...].astype(F32) - jnp.concatenate(totals, axis=0)
    out[2] = full_product(operand, inverse[0]).astype(BF16)


def row_exchange(partial):
    cores = lax.axis_size("core")
    chunks = partial.reshape((-1, cores) + partial.shape[1:])
    return lax.all_to_all(chunks, ("x", "y"), 0, 0, tiled=True)


def gather_column(copies):
    got = lax.all_to_all(copies, "zh", 0, 0, tiled=True)
    return got.reshape((-1,) + got.shape[2:])


def body(
    right_sides,
    lower_inverse,
    upper_inverse,
    lower_tiles,
    lower_source,
    lower_target,
    lower_rows,
    lower_count,
    upper_tiles,
    upper_source,
    upper_target,
    upper_rows,
    upper_count,
):
    sides = right_sides[0, 0, :, 0]
    low_inv, up_inv = lower_inverse[0, 0, :, 0], upper_inverse[0, 0, :, 0]
    low_tiles, up_tiles = lower_tiles[0, 0], upper_tiles[0, 0]
    low_rows, up_rows = lower_rows[0, 0], upper_rows[0, 0]
    low_source, low_target, low_count = lower_source[0, 0], lower_target[0, 0], lower_count[0, 0]
    up_source, up_target, up_count = upper_source[0, 0], upper_target[0, 0], upper_count[0, 0]
    side_extent, extent = sides.shape[1:]
    blocks = low_tiles.shape[1]
    pair, cores = lax.axis_size("zl"), lax.axis_size("core")
    high = lax.axis_size("zh")
    row_group = lax.axis_size("x") * lax.axis_size("y") * cores
    rows = side_extent // SPLIT
    tile_rows = blocks * extent

    first_sizes = [tile_rows, extent, side_extent, 8 * blocks]
    numbers = (low_source, low_target, low_count[None], up_source, up_target, up_count[None])
    packed, copies, forward_2 = pl.pallas_call(
        first_kernel,
        grid=(1,),
        in_specs=[one_of(sides, 1), one_of(sides, 2), one_of(low_inv, 1), one_of(low_inv, 2)]
        + [one_of(low_tiles, 0), one_of(low_rows, 0)]
        + [whole(array) for array in numbers],
        out_shape=[
            jax.ShapeDtypeStruct((sum(first_sizes), extent), BF16),
            jax.ShapeDtypeStruct((high, side_extent, extent), BF16),
            jax.ShapeDtypeStruct((side_extent, extent), BF16),
        ],
        out_specs=[
            pl.BlockSpec((sum(first_sizes), extent), lambda i: (0, 0)),
            pl.BlockSpec((high, side_extent, extent), lambda i: (0, 0, 0)),
            pl.BlockSpec((side_extent, extent), lambda i: (0, 0)),
        ],
        scratch_shapes=[pltpu.VMEM((8 * blocks, extent), jnp.int32)],
        compiler_params=pltpu.CompilerParams(vmem_limit_bytes=56 << 20),
    )(
        *(sides, sides, low_inv, low_inv, low_tiles, low_rows),
        *numbers,
    )
    z_mate = swapped(packed, "zl")
    copies = copies.reshape(-1, rows, extent)
    column = lax.all_to_all(copies, ("zh", "zl", "core"), 0, 0, tiled=True)
    column = column.reshape(-1, cores, rows, extent)
    packed, z_mate = lax.optimization_barrier((packed, z_mate))
    first = (packed, swapped(packed, "core"), z_mate, swapped(z_mate, "core"))

    later_sizes = [tile_rows] * 3 + [extent] * 3 + [side_extent]
    start = z_mate[:16]
    packed = pl.pallas_call(
        later_kernel,
        grid=(1,),
        in_specs=[one_of(sides, 0), one_of(low_inv, 0), one_of(up_inv, 0), one_of(up_inv, 1)]
        + [one_of(low_tiles, 1), whole(up_tiles), one_of(low_rows, 1), whole(up_rows), whole(start)],
        out_shape=jax.ShapeDtypeStruct((sum(later_sizes), extent), BF16),
        out_specs=pl.BlockSpec((sum(later_sizes), extent), lambda i: (0, 0)),
        compiler_params=pltpu.CompilerParams(vmem_limit_bytes=16 << 20),
    )(sides, low_inv, up_inv, up_inv, low_tiles, up_tiles, low_rows, up_rows, start)
    z_mate = swapped(packed, "zl")
    later = (packed, swapped(packed, "core"), z_mate, swapped(z_mate, "core"))

    def rows_of(sizes, number):
        start, size = sum(sizes[:number]), sizes[number]
        return pl.BlockSpec((size, extent), lambda i: (start // size, 0))

    place = jnp.stack([lax.axis_index("zl"), lax.axis_index("core")]).astype(jnp.int32)

    table = jnp.stack([buffer[-8 * blocks :, 0] for buffer in first])
    table = table.astype(F32).astype(jnp.int32)

    def edge(column, buffers, tile_block, group, level, before=None, by_target=False):
        shape = (row_group, pair) if not by_target else (pair, row_group)
        partial = jax.ShapeDtypeStruct(shape + (rows, extent), BF16)
        terms = jax.ShapeDtypeStruct((SPLIT, blocks, rows, extent), F32)
        extra = () if before is None else (before,)
        extra_specs = [whole(array) for array in extra]
        sums = (row_group + 1, pair) if not by_target else (pair, row_group + 1)
        return pl.pallas_call(
            functools.partial(scatter_kernel, group, level, by_target, before is not None),
            grid=(1,),
            in_specs=[whole(place), whole(table), whole(column)] + [tile_block] * SPLIT + extra_specs,
            out_shape=[partial, terms] if before is None else [partial],
            out_specs=[whole(partial), whole(terms)] if before is None else [whole(partial)],
            scratch_shapes=[pltpu.VMEM(sums + (rows, extent), F32)],
            compiler_params=pltpu.CompilerParams(vmem_limit_bytes=16 << 20),
        )(place, table, column, *buffers, *extra)

    def solve(kind, got, *pieces):
        solved = jax.ShapeDtypeStruct((SPLIT, rows, extent), BF16)
        copies = jax.ShapeDtypeStruct((high, pair, cores, rows, extent), BF16)
        arrays, specs = [], []
        for buffers, block in pieces:
            arrays += buffers
            specs += [block] * len(buffers)
        return pl.pallas_call(
            functools.partial(solve_kernel, kind),
            grid=(1,),
            in_specs=[whole(got)] + specs,
            out_shape=[solved, copies],
            out_specs=[whole(solved), whole(copies)],
            compiler_params=pltpu.CompilerParams(vmem_limit_bytes=16 << 20),
        )(got, *arrays)

    partial, terms = edge(column, first, rows_of(first_sizes, 0), 0, 1)
    got = row_exchange(partial)
    inverse, side = rows_of(first_sizes, 1), rows_of(first_sizes, 2)
    forward_1, copies = solve(0, got, (first, inverse), (first, side))
    column = gather_column(copies)
    (partial,) = edge(column, later, rows_of(later_sizes, 0), 1, 0, terms)
    got = row_exchange(partial)
    inverse, upper, side = (rows_of(later_sizes, i) for i in (3, 4, 6))
    solution_0, copies = solve(1, got, (later, inverse), (later, side), (later, upper))

    column = gather_column(copies)
    partial, terms = edge(column, later, rows_of(later_sizes, 1), 2, 0)
    got = row_exchange(partial)
    solution_1, copies = solve(2, got, (later, rows_of(later_sizes, 5)), ([forward_1], whole(forward_1)))
    column = gather_column(copies)

    done = jnp.stack([solution_0, solution_1], axis=1)
    home = [done[0]]
    for step in range(1, SPLIT):
        home.append(lax.ppermute(done[step], GROUP, [(i, i ^ step) for i in range(SPLIT)]))
    column, *home = lax.optimization_barrier((column, *home))
    (partial,) = edge(column, later, rows_of(later_sizes, 2), 3, 1, terms, by_target=True)
    got = lax.all_to_all(partial.reshape(-1, rows, extent), ("zl", "x", "y", "core"), 0, 0, tiled=True)
    got = got.reshape(pair, row_group // cores, cores, rows, extent)
    result = jax.ShapeDtypeStruct(sides.shape, BF16)
    result = pl.pallas_call(
        last_kernel,
        grid=(1,),
        in_specs=[whole(got), whole(forward_2), one_of(up_inv, 2)]
        + [whole(piece) for piece in home],
        out_shape=result,
        out_specs=whole(result),
        compiler_params=pltpu.CompilerParams(vmem_limit_bytes=16 << 20),
    )(got, forward_2, up_inv, *home)
    return result[None, None, :, None]


def solution(mesh):
    z_extent = mesh.shape["prow"]
    grid = mesh.devices.reshape(z_extent // 2, 2, 4, 4, 2)
    split_mesh = Mesh(grid, ("zh", "zl", "x", "y", "core"))
    row, col = ("zh", "zl"), ("x", "y", "core")
    ranks = (6, 6, 6, 6, 4, 4, 5, 3, 6, 4, 4, 5, 3)
    placed = tuple(P(row, col, *([None] * (rank - 2))) for rank in ranks)
    return jax.shard_map(
        body,
        mesh=split_mesh,
        in_specs=placed,
        out_specs=P(row, col, None, None, None, None),
        check_vma=False,
    )
```
